32 devices in a mesh: section: 2 (over core), dp: 8 (over z, x), rep: 2 (over y).
Axes of the slice: x: 2, y: 2, z: 4, core: 2. Of those that a mesh axis runs over, the one named last changes fastest.
Arguments:
- past_values: bfloat16 [32768, 336], P(('dp', 'rep')), may hold values from -6 to 6
- horizon_label: int32 [32768], P(('dp', 'rep')), may hold values from 0 to 3, as said below
- lookback_observed: int32 [32768, 336], P(('dp', 'rep')), may hold values from 0 to 1, as said below
- prediction_scored: int32 [32768, 64], P(('dp', 'rep')), may hold values from 0 to 1, as said below
- adjoint_prediction: bfloat16 [32768, 64], P(('dp', 'rep')), may hold values from -6 to 6
- adjoint_leftover: bfloat16 [32768, 336], P(('dp', 'rep')), may hold values from -6 to 6
- entry_matrix: bfloat16 [2, 336, 512], P('section'), may hold values from -0.3125 to 0.3125
- inner_matrices: bfloat16 [2, 3, 512, 512], P('section'), may hold values from -0.25 to 0.25
- coefficient_matrices: bfloat16 [2, 2, 512, 512], P('section'), may hold values from -0.25 to 0.25
- lookback_basis: bfloat16 [2, 512, 336], P('section'), may hold values from -0.25 to 0.25
- prediction_basis: bfloat16 [2, 512, 256], P('section'), may hold values from -0.25 to 0.25
- inner_offsets: float32 [2, 6, 512], P('section'), may hold values from -2 to 2
- lookback_offset: float32 [2, 336], P('section'), may hold values from -2 to 2
- prediction_offset: float32 [2, 256], P('section'), may hold values from -2 to 2
Outputs:
- prediction_pair: float32 [2, 32768, 64], P('section', ('dp', 'rep'))
- outcome_pair: float32 [2, 32768, 336], P('section', ('dp', 'rep'))
- grad_first: float32 [2, 336, 512], P('section')
- grad_mid: float32 [2, 3, 512, 512], P('section')
- grad_theta: float32 [2, 2, 512, 512], P('section')
- grad_back: float32 [2, 512, 336], P('section')
- grad_fore: float32 [2, 512, 256], P('section')
- grad_hidden_bias: float32 [2, 6, 512], P('section')
- grad_back_bias: float32 [2, 336], P('section')
- grad_fore_bias: float32 [2, 256], P('section')
The draws below stay inside these ranges and needn't reach their ends.
Inputs may be any that keep to these rules, and one draw needn't show every extreme that they name: `horizon_label`: group g has horizon 6, 8, 18 or 48 for g = 0, 1, 2, 3. `lookback_observed`: ones only in the last 7 h positions, h the window's horizon. `prediction_scored`: ones only in the first h positions, h the window's horizon.
All inputs are finite; a program needn't handle non-finite values.
Results may differ from the reference program's by a relative error of at most 0.014.
Values may be sent and summed in bfloat16 or wider, within the bound.
A program may use at most 192 MiB of HBM per device.

```python
import math
import jax
import jax.numpy as jnp
from jax import lax

UNIT_COUNT = 512
L = 336
OUTLOOK_SPAN = 64
HORIZON_SETS = 4
SAMPLE_COUNT = 32768


def group_draw(key):
    return jax.random.randint(key, (SAMPLE_COUNT,), 0, HORIZON_SETS).astype(jnp.int32)


def horizon_of(horizon_sets):
    table = jnp.array([6, 8, 18, 48], dtype=jnp.int32)
    return jnp.sum(jnp.where(horizon_sets[:, None] == jnp.arange(4, dtype=jnp.int32)[None, :], table[None, :], 0), axis=1)


def draw_horizon_label(key, part):
    shared = group_draw(key)
    return shared


def draw_lookback_observed(key, part):
    shared = group_draw(key)
    key = jax.random.fold_in(key, 2)
    needed = 7 * horizon_of(shared)
    location = jnp.arange(L, dtype=jnp.int32)
    inside = location[None, :] >= (L - needed)[:, None]
    visited_items = jax.random.randint(key, (SAMPLE_COUNT, L), 0, 10) > 0
    return (inside & visited_items).astype(jnp.int32)


def draw_prediction_scored(key, part):
    shared = group_draw(key)
    key = jax.random.fold_in(key, 3)
    reach = horizon_of(shared)
    location = jnp.arange(OUTLOOK_SPAN, dtype=jnp.int32)
    inside = location[None, :] < reach[:, None]
    visited_items = jax.random.randint(key, (SAMPLE_COUNT, OUTLOOK_SPAN), 0, 10) > 0
    return (inside & visited_items).astype(jnp.int32)


def steps_of(own_key, extent, cuts, least, high):
    loudness = 1.0
    for dim, parts in cuts:
        steps = jax.random.uniform(jax.random.fold_in(jax.random.fold_in(own_key, 6), dim), (parts,), jnp.float32, least / len(cuts), high / len(cuts))
        loudness = loudness * jnp.repeat(jnp.exp(steps), extent[dim] // parts).reshape((-1,) + (1,) * (len(extent) - 1 - dim))
    return loudness


def bell_draw(own_key, shape, deviation, most, cuts=(), held_as=jnp.bfloat16):
    values = jax.random.normal(own_key, shape, jnp.float32) * deviation
    if len(cuts) > 0:
        values = steps_of(own_key, shape, cuts, -0.22, 0.18) * values
    return jnp.clip(values, min=-most, max=most).astype(held_as)


def setup_inputs(seed: int = 0) -> dict:
    key_of = jax.random.split(jax.random.key(seed), 15)
    past_values = bell_draw(key_of[0], (SAMPLE_COUNT, L), 1.0, 6.0, ((0, 16),))
    horizon_label = draw_horizon_label(jax.random.fold_in(key_of[14], 71), 0)
    lookback_observed = draw_lookback_observed(jax.random.fold_in(key_of[14], 71), 0)
    prediction_scored = draw_prediction_scored(jax.random.fold_in(key_of[14], 71), 0)
    adjoint_prediction = bell_draw(key_of[4], (SAMPLE_COUNT, OUTLOOK_SPAN), 1.0, 6.0, ((0, 16),))
    adjoint_leftover = bell_draw(key_of[5], (SAMPLE_COUNT, L), 1.0, 6.0, ((0, 16),))
    entry_matrix = bell_draw(key_of[6], (2, L, UNIT_COUNT), L ** -0.5, 0.3125, ((0, 2),))
    inner_matrices = bell_draw(key_of[7], (2, 3, UNIT_COUNT, UNIT_COUNT), UNIT_COUNT ** -0.5, 0.25, ((0, 2),))
    coefficient_matrices = bell_draw(key_of[8], (2, 2, UNIT_COUNT, UNIT_COUNT), UNIT_COUNT ** -0.5, 0.25, ((0, 2),))
    lookback_basis = bell_draw(key_of[9], (2, UNIT_COUNT, L), UNIT_COUNT ** -0.5, 0.25, ((0, 2),))
    prediction_basis = bell_draw(key_of[10], (2, UNIT_COUNT, HORIZON_SETS * OUTLOOK_SPAN), UNIT_COUNT ** -0.5, 0.25, ((0, 2),))
    inner_offsets = bell_draw(key_of[11], (2, 6, UNIT_COUNT), 0.3, 2.0, ((0, 2),), jnp.float32)
    lookback_offset = bell_draw(key_of[12], (2, L), 0.3, 2.0, ((0, 2),), jnp.float32)
    prediction_offset = bell_draw(key_of[13], (2, HORIZON_SETS * OUTLOOK_SPAN), 0.3, 2.0, ((0, 2),), jnp.float32)
    return {"past_values": past_values, "horizon_label": horizon_label, "lookback_observed": lookback_observed, "prediction_scored": prediction_scored, "adjoint_prediction": adjoint_prediction, "adjoint_leftover": adjoint_leftover, "entry_matrix": entry_matrix, "inner_matrices": inner_matrices, "coefficient_matrices": coefficient_matrices, "lookback_basis": lookback_basis, "prediction_basis": prediction_basis, "inner_offsets": inner_offsets, "lookback_offset": lookback_offset, "prediction_offset": prediction_offset}


@jax.custom_vjp
def low(v):
    return lax.optimization_barrier(v.astype(jnp.bfloat16)).astype(jnp.float32)

@jax.custom_vjp
def low_back(v):
    return v

def low_keep(v):
    return (low(v), None)

def low_pass(kept, grad):
    return (grad,)

def back_keep(v):
    return (v, None)

def back_low(kept, grad):
    return (low(grad),)
low.defvjp(low_keep, low_pass)
low_back.defvjp(back_keep, back_low)

def matmul(left, right):
    return jnp.dot(left, right, precision=lax.Precision.HIGHEST)

def one_block(values, look_mask, hor_mask, onehot, weights):
    first_w, mid_w, theta_w, back_w, fore_w, hidden_b, back_b, fore_b = weights
    inside = values * look_mask
    hidden = low(inside)
    preact = low_back(matmul(hidden, first_w) + hidden_b[0])
    hidden = low(jax.nn.silu(preact))
    for depth in range(3):
        preact = low_back(matmul(hidden, mid_w[depth]) + hidden_b[depth + 1])
        hidden = low(jax.nn.silu(preact))
    theta_back = low(low_back(matmul(hidden, theta_w[0]) + hidden_b[4]))
    theta_fore = low(low_back(matmul(hidden, theta_w[1]) + hidden_b[5]))
    backcast = low_back(matmul(theta_back, back_w) + back_b)
    output_values = low_back(matmul(theta_fore, fore_w) + fore_b)
    output_values = output_values.reshape(output_values.shape[0], HORIZON_SETS, OUTLOOK_SPAN)
    partial_value = lax.optimization_barrier(jnp.sum(output_values * onehot[:, :, None], axis=1)) * hor_mask
    return ((inside - backcast) * look_mask, partial_value)

def two_blocks(values, weights, look_mask, hor_mask, onehot):
    block_zero = tuple((w[0] for w in weights))
    block_one = tuple((w[1] for w in weights))
    residual, partial_value = one_block(values, look_mask, hor_mask, onehot, block_zero)
    resid_sent = low(low_back(residual))
    fore_sent = low(partial_value)
    final_res, second_part = one_block(resid_sent, look_mask, hor_mask, onehot, block_one)
    return ((fore_sent + second_part, final_res), fore_sent)

def reference(past_values, horizon_label, lookback_observed, prediction_scored, adjoint_prediction, adjoint_leftover, entry_matrix, inner_matrices, coefficient_matrices, lookback_basis, prediction_basis, inner_offsets, lookback_offset, prediction_offset):
    parameter_set = tuple((parameter_entry.astype(jnp.float32) for parameter_entry in (entry_matrix, inner_matrices, coefficient_matrices, lookback_basis, prediction_basis, inner_offsets, lookback_offset, prediction_offset)))
    block_rows = math.gcd(SAMPLE_COUNT, 4096)
    block_count = SAMPLE_COUNT // block_rows

    def each_unit(a):
        return a.reshape((block_count, block_rows) + a.shape[1:])
    unit_sequence = (each_unit(past_values.astype(jnp.float32)), each_unit(horizon_label), each_unit(lookback_observed.astype(jnp.float32)), each_unit(prediction_scored.astype(jnp.float32)), each_unit(adjoint_prediction.astype(jnp.float32)), each_unit(adjoint_leftover.astype(jnp.float32)))

    def carry_onward(cumulative_sums, slices):
        values, group_rows, look_mask, hor_mask, cot_fore, cot_resid = slices
        onehot = (group_rows[:, None] == jnp.arange(HORIZON_SETS, dtype=jnp.int32)[None, :]).astype(jnp.float32)

        def wrapped(inputs, *weights):
            return two_blocks(inputs, weights, look_mask, hor_mask, onehot)
        results, pullback, fore_sent = jax.vjp(wrapped, values, *parameter_set, has_aux=True)
        gradients = pullback((cot_fore, cot_resid))
        cumulative_sums = tuple((a + b for a, b in zip(cumulative_sums, gradients[1:])))
        return (cumulative_sums, (fore_sent, results[0], results[1], gradients[0]))
    empty_derivatives = tuple((jnp.zeros_like(parameter_entry) for parameter_entry in parameter_set))
    cumulative_sums, (shares_passed, prediction_sums, closing_values, source_derivatives) = lax.scan(carry_onward, empty_derivatives, unit_sequence)

    def linearize_structure(a):
        return a.reshape((SAMPLE_COUNT,) + a.shape[2:])
    prediction_pair = jnp.stack([linearize_structure(shares_passed), linearize_structure(prediction_sums)])
    outcome_pair = jnp.stack([linearize_structure(source_derivatives), linearize_structure(closing_values)])
    return (prediction_pair, outcome_pair, cumulative_sums[0], cumulative_sums[1], cumulative_sums[2], cumulative_sums[3], cumulative_sums[4], cumulative_sums[5], cumulative_sums[6], cumulative_sums[7])
```

```python
import functools
from typing import Any, NamedTuple

import jax
import jax.numpy as jnp
from jax import lax
from jax.experimental import pallas as pl
from jax.experimental.pallas import tpu as pltpu
from jax.sharding import PartitionSpec as P

BF16 = jnp.bfloat16
F32 = jnp.float32
MESH = pl.DeviceIdType.MESH

BACK, FORE, TB, TF, M0, M1, M2, FIRST = range(8)
PIECE_ROWS = (384, 256, 512, 512, 512, 512, 512, 384)
ROUNDS = (
    (0, (TF,)),
    (1, (TB, TF)),
    (1, (M2,)),
    (1, (M1,)),
    (1, (M0,)),
    (1, (FIRST,)),
    (1, (BACK, FORE)),
    (0, (BACK, FORE, TB)),
    (0, (M2,)),
    (0, (M1,)),
    (0, (M0,)),
    (0, (FIRST,)),
)
D2D, S1, S2, S3, S4, G3, G2, G1, G1X, GD = range(10)
LANDING = (1, 2, 4, 8, 8)
(
    LOAD, Z1_0, Z2_0, Z3_0, Z4_0, GH_0, GTF_0, BACK_0, Z1_1, Z2_1, Z3_1, Z4_1, PP_1, GT_1, DH4_1,
    B3_1, B2_1, B1_1, B0_1, GB_0, GTB_0, DH4_0, B3_0, B2_0, B1_0, B0_0, HEADS_0, THETA_1, FINAL_1,
) = range(29)
STEP = 1000
ORDER = (
    LOAD, Z1_0, Z2_0, Z3_0, Z4_0, GH_0, GTF_0, BACK_0, Z1_1, 1000, Z2_1, Z3_1, Z4_1, PP_1, GT_1, 1001, DH4_1,
    B3_1, 1010, B2_1, 1002, 1020, B1_1, 1030, B0_1, 1040, GB_0, 1003, 1011, 1050, 1021, HEADS_0, 1031, GTB_0,
    1041, DH4_0, 1004, 1051, 1070, B3_0, 1012, B2_0, 1005, 1022, 1032, 1080, B1_0, 1042, 1052, 1071, 1090,
    1013, 1023, B0_0, 1006, 1033, 1043, 1053, 1081, 1100, 1110, THETA_1, 1072, 1007, 1091, FINAL_1, 1060,
    1014, 1101, 1111, 1024, 1034, 1073, 1044, 1054, 1082, 1092, 1061, 1015, 1102, 1025, 1035, 1045, 1055,
    1112, 1083, 1093, 1103, 1074, 1062, 1113, 1016, 1075, 1063, 1026, 1036, 1046, 1056, 1017, 1027, 1084,
    1094, 1037, 1104, 1114, 1047, 1057, 1076, 1085, 1095, 1105, 1115, 1064, 1086, 1096, 1077, 1065, 1106,
    1116, 1087, 1097, 1066, 1107, 1117, 1067,
)


def rows_of(number):
    return sum(PIECE_ROWS[piece] for piece in ROUNDS[number][1])


def place_of(block, piece):
    for number, (at, pieces) in enumerate(ROUNDS):
        if at == block and piece in pieces:
            return number, sum(PIECE_ROWS[p] for p in pieces[: pieces.index(piece)])


def nn(a, b):
    return jnp.dot(a, b, preferred_element_type=F32)


def nt(a, b):
    return lax.dot_general(a, b, (((1,), (1,)), ((), ())), preferred_element_type=F32)


def tn(a, b):
    return lax.dot_general(a, b, (((0,), (0,)), ((), ())), preferred_element_type=F32)


class Inputs(NamedTuple):
    past: Any
    look: Any
    label: Any
    scored: Any
    adjp: Any
    adjl: Any


class Given(NamedTuple):
    first: Any
    mid: Any
    theta: Any
    back: Any
    fore: Any
    hid: Any
    backb: Any
    foreb: Any


class Results(NamedTuple):
    pair: Any
    outcome: Any
    first: Any
    mid: Any
    theta: Any
    back: Any
    fore: Any


class Weights(NamedTuple):
    first: Any
    hid: Any
    mid0: Any
    mid1: Any
    mid2: Any
    theta_b: Any
    theta_f: Any
    back: Any
    backb: Any
    fore: Any
    foreb: Any


class Block(NamedTuple):
    h: Any
    d: Any
    gb: Any
    pp: Any
    bias: Any
    hid: Any
    backb: Any
    foreb: Any


class Round(NamedTuple):
    part: Any
    landing: Any
    rest: Any


class Scratch(NamedTuple):
    weights: Any
    blocks: Any
    rounds: Any
    observed: Any
    mask: Any
    label: Any
    scored: Any
    adjp: Any
    gh: Any
    tt: Any
    sent: Any
    total: Any
    dinput: Any
    r2: Any
    load_sem: Any
    weight_sem: Any
    weight_send: Any
    send_sem: Any
    recv_sem: Any
    out_sem: Any
    give_send: Any
    give_recv: Any


def scratch(n):
    def weights():
        square = pltpu.VMEM((512, 512), BF16)
        return Weights(
            first=pltpu.VMEM((336, 512), BF16),
            hid=pltpu.VMEM((24, 128), F32),
            mid0=square,
            mid1=square,
            mid2=square,
            theta_b=square,
            theta_f=square,
            back=pltpu.VMEM((336, 512), BF16),
            backb=pltpu.VMEM((1, 336), F32),
            fore=pltpu.VMEM((512, 256), BF16),
            foreb=pltpu.VMEM((1, 256), F32),
        )

    def block():
        return Block(
            h=[pltpu.VMEM(((336 if k == 0 else 512) + 16, n), BF16) for k in range(5)],
            d=[pltpu.VMEM((512, n), BF16) for _ in range(4)],
            gb=pltpu.VMEM((336, n), BF16),
            pp=pltpu.VMEM((1024, n), BF16),
            bias=pltpu.VMEM((16, 512), F32),
            hid=pltpu.VMEM((512, 8), F32),
            backb=pltpu.VMEM((336, 8), F32),
            foreb=pltpu.VMEM((256, 8), F32),
        )

    def a_round(number):
        rows = rows_of(number)
        half = rows // 2

        def landing(portion):
            shape = (half // portion, 512)
            return pltpu.VMEM(shape if shape[0] % 16 == 0 else (2 * shape[0], 256), BF16)

        return Round(
            part=pltpu.VMEM((rows, 512), BF16),
            landing=[landing(portion) for portion in LANDING],
            rest=pltpu.VMEM((half, 512), BF16),
        )

    dma = pltpu.SemaphoreType.DMA
    count = len(ROUNDS)
    return Scratch(
        weights=[weights(), weights()],
        blocks=[block(), block()],
        rounds=[a_round(number) for number in range(count)],
        observed=pltpu.VMEM((336, n), jnp.int32),
        mask=pltpu.VMEM((336, n), BF16),
        label=pltpu.VMEM((n // 128, 128), jnp.int32),
        scored=pltpu.VMEM((64, n), jnp.int32),
        adjp=pltpu.VMEM((64, n), BF16),
        gh=pltpu.VMEM((256, n), BF16),
        tt=pltpu.VMEM((1024, n), BF16),
        sent=pltpu.VMEM((64, n), BF16),
        total=pltpu.VMEM((64, n), BF16),
        dinput=pltpu.VMEM((336, n), BF16),
        r2=pltpu.VMEM((336, n), BF16),
        load_sem=dma((6,)),
        weight_sem=dma((2, 11)),
        weight_send=dma((2, 11)),
        send_sem=dma((count, 10)),
        recv_sem=dma((count, 10)),
        out_sem=dma((2 * 8, 4)),
        give_send=dma((4,)),
        give_recv=dma((4,)),
    )


def body(n, whole, treedef, *refs):
    inputs, given, outs, s = jax.tree.unflatten(treedef, refs)
    weights, blocks, rounds = s.weights, s.blocks, s.rounds

    c = lax.axis_index("section")
    dp = lax.axis_index("dp")
    y = lax.axis_index("rep")
    z = lax.div(dp, 2)
    x = lax.rem(dp, 2)
    other = 1 - c
    dpx = dp + 1 - 2 * x
    dpz = dp + 2 - 4 * lax.rem(z, 2)
    dpm = 2 * (3 - z) + x
    ry = 1 - y
    dp1 = jnp.where(c == 0, dpx, dp)
    rep1 = jnp.where(c == 0, y, ry)
    dp2 = jnp.where(c == 0, dp, dpx)
    rep2 = jnp.where(c == 0, ry, y)
    bits = (jnp.where(c == 0, x, y), lax.rem(lax.div(z + 1, 2), 2), jnp.where(c == 0, y, x))

    mine = pl.ds(pl.multiple_of(c * n, 128), n)
    label_rows = n // 128
    loads = Inputs(
        past=(inputs.past.at[:, mine], blocks[0].h[0].at[pl.ds(0, 336)]),
        look=(inputs.look.at[:, mine], s.observed),
        label=(inputs.label.at[pl.ds(pl.multiple_of(c * label_rows, 8), label_rows)], s.label),
        scored=(inputs.scored.at[:, mine], s.scored),
        adjp=(inputs.adjp.at[:, mine], s.adjp),
        adjl=(inputs.adjl.at[:, mine], blocks[1].gb),
    )
    loads = Inputs(*(pltpu.make_async_copy(*pair, s.load_sem.at[i]) for i, pair in enumerate(loads)))
    sources = Weights(
        first=given.first.at[0],
        hid=given.hid,
        mid0=given.mid.at[0, 0],
        mid1=given.mid.at[0, 1],
        mid2=given.mid.at[0, 2],
        theta_b=given.theta.at[0, 0],
        theta_f=given.theta.at[0, 1],
        back=given.back,
        backb=given.backb,
        fore=given.fore.at[0],
        foreb=given.foreb,
    )

    def weight_local(block, i):
        return pltpu.make_async_copy(sources[i], weights[block][i], s.weight_sem.at[block, i])

    def weight_remote(block, i):
        return pltpu.make_async_remote_copy(
            sources[i],
            weights[block][i],
            s.weight_send.at[block, i],
            s.weight_sem.at[block, i],
            device_id=(other, dp, y),
            device_id_type=MESH,
        )

    names = Weights(*range(11))

    waited = set()

    def wait_weights(block, *keys):
        for key in keys:
            if (block, key) not in waited:
                waited.add((block, key))
                weight_local(block, key).wait()

    def regions(number, base):
        n1 = rows_of(number) // 4

        def at(start, count, col=0, width=512):
            if width == 512:
                return (pl.ds(pl.multiple_of(start, 16), count), slice(None))
            return (pl.ds(pl.multiple_of(start, 16), count), pl.ds(pl.multiple_of(col, 128), width))

        start1 = base + bits[0] * n1
        start2 = start1 + bits[1] * (n1 // 2)
        keep = [at(base, 2 * n1), at(start1, n1), at(start2, n1 // 2)]
        give = [None, at(base + (1 - bits[0]) * n1, n1), at(start1 + (1 - bits[1]) * (n1 // 2), n1 // 2)]
        n3 = n1 // 4
        if n3 % 16 == 0:
            keep.append(at(start2 + bits[2] * n3, n3))
            give.append(at(start2 + (1 - bits[2]) * n3, n3))
        else:
            keep.append(at(start2, n1 // 2, bits[2] * 256, 256))
            give.append(at(start2, n1 // 2, (1 - bits[2]) * 256, 256))
        return keep, give

    def summed(number):
        return regions(number, c * (rows_of(number) // 2))

    def message(number, kind):
        r = rounds[number]
        half = rows_of(number) // 2
        device = (
            (other, dp, y),
            (c, dp1, rep1),
            (c, dpz, y),
            (c, dp2, rep2),
            (c, dpm, y),
            (c, dp2, rep2),
            (c, dpz, y),
            (c, dp1, rep1),
            (other, dp1, rep1),
            (other, dp, y),
        )[kind]
        if kind <= S4:
            keep, give = summed(number)
            where = (
                (pl.ds(pl.multiple_of(other * half, 16), half), slice(None)),
                give[1],
                give[2],
                give[3],
                keep[3],
            )[kind]
            src, dst = r.part.at[where], r.landing[kind]
        else:
            keep, _ = regions(number, 0)
            where = keep[(3, 2, 1, 1, 1 if whole else 0)[kind - G3]]
            src = r.landing[D2D].at[where]
            dst = src if kind <= G1 else r.rest.at[where]
        return pltpu.make_async_remote_copy(
            src,
            dst,
            s.send_sem.at[number, kind],
            s.recv_sem.at[number, kind],
            device_id=device,
            device_id_type=MESH,
        )

    def fold(number, kind, where, *buffer):
        part = rounds[number].part
        part[where] = part[where] + rounds[number].landing[kind][buffer]

    def fold_and_send(number, kind):
        keep, give = summed(number)
        level = kind + 1
        bit = bits[kind]
        rows, cols = rounds[number].landing[kind].shape

        def of_landing(side):
            if rows // 2 % 16 == 0:
                return (pl.ds(pl.multiple_of(side * (rows // 2), 16), rows // 2), slice(None))
            return (slice(None), pl.ds(pl.multiple_of(side * (cols // 2), 128), cols // 2))

        fold(number, kind, give[level], *of_landing(1 - bit))
        message(number, level).start()
        fold(number, kind, keep[level], *of_landing(bit))

    def settle(number, kind, level):
        r = rounds[number]
        here = regions(number, 0)[0][level]
        r.landing[D2D][here] = r.part[summed(number)[0][level]] + r.landing[kind][...]

    def deliver(number):
        block, pieces = ROUNDS[number]
        half = rows_of(number) // 2
        copies = []
        first = 0
        for piece in pieces:
            count = (336, 256, 512, 512, 512, 512, 512, 352)[piece]
            out = (outs.back, None, outs.theta.at[0], outs.theta.at[1], *(outs.mid.at[k] for k in range(3)), outs.first)
            used = 0
            for side in range(2):
                low, high = max(first, side * half), min(first + count, (side + 1) * half)
                if low >= high:
                    continue
                held = rounds[number].landing[D2D] if side == block else rounds[number].rest
                src = held.at[pl.ds(low - side * half, high - low)]
                if piece == FORE:
                    ways = [
                        (src.at[:, pl.ds(256 * k, 256)], outs.fore.at[pl.ds(256 * k + low - first, high - low)])
                        for k in range(2)
                    ]
                else:
                    ways = [(src, out[piece].at[pl.ds(low - first, high - low)])]
                for way in ways:
                    copies.append(pltpu.make_async_copy(*way, s.out_sem.at[8 * block + piece, used]))
                    used += 1
            first += PIECE_ROWS[piece]
        return copies

    def chip_step(number):
        block = ROUNDS[number][0]
        message(number, D2D).wait_recv()
        settle_half(number)
        pl.when(c != block)(lambda: message(number, GD).start())

        @pl.when(c == block)
        def _():
            message(number, GD).wait_recv()
            for copy in deliver(number):
                copy.start()

    def settle_half(number):
        r = rounds[number]
        r.landing[D2D][...] = r.landing[D2D][...] + r.part[summed(number)[0][0]]

    def step(number, kind):
        block = ROUNDS[number][0]
        if kind < G1:
            message(number, kind).wait_recv()
        if kind < S3:
            fold_and_send(number, kind)
        elif kind == S3:
            fold(number, kind, summed(number)[0][3], ...)
            message(number, S4).start()
        elif kind == S4:
            settle(number, kind, 3)
            message(number, G3).start()
        elif kind == G3:
            message(number, G2).start()
        elif kind == G2:
            pl.when(c == block)(lambda: message(number, G1).start())

            @pl.when(c != block)
            def _():
                message(number, G1X).start()
                message(number, GD).start()
        else:

            @pl.when(c == block)
            def _():
                quarter = rows_of(number) // 4
                for kind, ref, side in (
                    (G1, rounds[number].landing[D2D], 1 - bits[0]),
                    (GD, rounds[number].rest, bits[2]),
                    (G1X, rounds[number].rest, 1 - bits[2]),
                ):
                    ref = ref.at[pl.ds(pl.multiple_of(side * quarter, 16), quarter)]
                    pltpu.make_async_remote_copy(
                        ref,
                        ref,
                        s.send_sem.at[number, kind],
                        s.recv_sem.at[number, kind],
                        device_id=(other, dp, y),
                        device_id_type=MESH,
                    ).wait_recv()
                for copy in deliver(number):
                    copy.start()

    def wait_sends():
        for number, (block, _) in enumerate(ROUNDS):
            for kind in (D2D, S1, S2, S3, S4, G3, G2) if whole else (D2D,):
                message(number, kind).wait_send()
            if whole:
                pl.when(c == block)(lambda number=number: message(number, G1).wait_send())
                pl.when(c != block)(lambda number=number: message(number, G1X).wait_send())
            pl.when(c != block)(lambda number=number: message(number, GD).wait_send())

    def result(i):
        src = (s.sent, s.total, s.dinput, s.r2)[i]
        dst = (outs.pair, outs.outcome)[i // 2].at[:, mine]
        local = pltpu.make_async_copy(src, dst, s.give_send.at[i])
        remote = pltpu.make_async_remote_copy(
            src, dst, s.give_send.at[i], s.give_recv.at[i], device_id=(other, dp, y), device_id_type=MESH
        )
        return i % 2, local, remote

    def hand_over(i):
        keeper, local, remote = result(i)
        pl.when(c == keeper)(lambda: local.start())
        pl.when(c != keeper)(lambda: remote.start())

    def handed_over():
        for i in range(4):
            keeper, local, remote = result(i)

            @pl.when(c == keeper)
            def _(local=local, remote=remote):
                local.wait()
                remote.wait_recv()

            pl.when(c != keeper)(lambda remote=remote: remote.wait_send())

    missing = [set(pieces) for _, pieces in ROUNDS]

    def store(block, piece, value):
        number, first = place_of(block, piece)
        missing[number].discard(piece)
        value = value.astype(BF16)
        part = rounds[number].part
        if piece == FORE:
            for k in range(2):
                part[first : first + 256, 256 * k : 256 * (k + 1)] = value[256 * k : 256 * (k + 1)]
        else:
            part[first : first + value.shape[0], :] = value

    def store_with_bias(block, piece, value, row):
        k = value.shape[0] - 16
        blocks[block].bias[row : row + 1, :] = value[k : k + 1]
        store(block, piece, value[:k])

    def row_sums(block, row, value):
        folded = value[:, 0:128]
        for i in range(1, n // 128):
            folded = folded + value[:, 128 * i : 128 * (i + 1)]
        sums = nt(jnp.ones((16, 128), BF16), folded.astype(BF16))
        blocks[block].bias[row : row + 1, 0 : value.shape[0]] = sums[0:1]

    def layer(block, depth):
        b, w = blocks[block], weights[block]
        h = b.h[depth - 1]
        zed = tn(w[(names.first, names.mid0, names.mid1, names.mid2)[depth - 1]][...], h[0 : h.shape[0] - 16, :])
        zed = zed + b.hid[:, depth - 1 : depth]
        sig = 0.5 * jnp.tanh(0.5 * zed) + 0.5
        out = zed * sig
        b.h[depth][0:512, :] = out.astype(BF16)
        b.d[depth - 1][...] = (sig + out * (1.0 - sig)).astype(BF16)

    def theta(block, k):
        w = weights[block][names.theta_b + k]
        return (tn(w[...], blocks[block].h[4][0:512, :]) + blocks[block].hid[:, 4 + k : 5 + k]).astype(BF16)

    def heads(block, theta_f):
        wide = tn(weights[block].fore[...], theta_f) + blocks[block].foreb[:, 0:1]
        row = label_row()
        chosen = jnp.zeros((64, n), F32)
        for g in range(4):
            chosen = chosen + jnp.where(row == g, wide[64 * g : 64 * (g + 1)], 0.0)
        return chosen * s.scored[...].astype(F32)

    def residual(block, theta_b):
        backcast = nn(weights[block].back[...], theta_b) + blocks[block].backb[:, 0:1]
        return (blocks[block].h[0][0:336, :].astype(F32) - backcast) * s.mask[...].astype(F32)

    def inward(block, depth, dh):
        d = blocks[block].d[depth - 1]
        d[...] = (dh * d[...].astype(F32)).astype(BF16)

    def layer_biases(block):
        b, w = blocks[block], weights[block]
        lines = [
            jnp.concatenate([w.hid[4 * k + i : 4 * k + i + 1, :] for i in range(4)], axis=1) for k in range(6)
        ]
        lines.append(jnp.zeros((2, 512), F32))
        b.hid[...] = jnp.concatenate(lines, axis=0).T

    def end_biases(block):
        b, w = blocks[block], weights[block]
        wait_weights(block, names.backb, names.foreb)
        b.backb[...] = jnp.broadcast_to(w.backb[...], (8, 336)).T
        b.foreb[...] = jnp.broadcast_to(w.foreb[...], (8, 256)).T

    def label_row():
        return jnp.concatenate([s.label[i : i + 1, :] for i in range(label_rows)], axis=1)

    def run(task):
        one, two = blocks
        if task == LOAD:
            loads.look.wait()
            mask = s.observed[...].astype(F32).astype(BF16)
            s.mask[...] = mask
            loads.past.wait()
            one.h[0][0:336, :] = one.h[0][0:336, :] * mask
            for b in blocks:
                for h in b.h:
                    k = h.shape[0] - 16
                    h[k : k + 16, :] = jnp.ones((16, n), BF16)
                b.bias[...] = jnp.zeros((16, 512), F32)
            wait_weights(0, names.hid)
            layer_biases(0)
        elif task in (Z1_0, Z2_0, Z3_0, Z4_0):
            depth = task - Z1_0 + 1
            wait_weights(0, (names.first, names.mid0, names.mid1, names.mid2)[depth - 1])
            layer(0, depth)
        elif task in (Z1_1, Z2_1, Z3_1, Z4_1):
            depth = task - Z1_1 + 1
            if depth == 1:
                wait_weights(1, names.hid)
                layer_biases(1)
            wait_weights(1, (names.first, names.mid0, names.mid1, names.mid2)[depth - 1])
            layer(1, depth)
        elif task == GH_0:
            wait_weights(0, names.fore)
            for load in (loads.label, loads.scored, loads.adjp):
                load.wait()
            df = s.adjp[...].astype(F32) * s.scored[...].astype(F32)
            row = label_row()
            gh = jnp.concatenate([jnp.where(row == g, df, 0.0) for g in range(4)], axis=0)
            s.gh[...] = gh.astype(BF16)
            for block in range(2):
                row_sums(block, 7, gh)
            one.pp[512:1024, :] = nn(weights[0].fore[...], s.gh[...]).astype(BF16)
        elif task == GTF_0:
            store_with_bias(0, TF, nt(one.h[4][...], one.pp[512:1024, :]), 5)
        elif task == BACK_0:
            wait_weights(0, names.theta_b, names.back)
            end_biases(0)
            theta_b = theta(0, 0)
            one.pp[0:512, :] = theta_b
            two.h[0][0:336, :] = residual(0, theta_b).astype(BF16)
        elif task == PP_1:
            wait_weights(1, names.back, names.fore)
            loads.adjl.wait()
            gb = -(two.gb[...] * s.mask[...])
            two.gb[...] = gb
            row_sums(1, 6, gb.astype(F32))
            two.pp[0:512, :] = tn(weights[1].back[...], gb).astype(BF16)
            two.pp[512:1024, :] = nn(weights[1].fore[...], s.gh[...]).astype(BF16)
        elif task == GT_1:
            for k in range(2):
                store_with_bias(1, (TB, TF)[k], nt(two.h[4][...], two.pp[512 * k : 512 * (k + 1), :]), 4 + k)
        elif task in (DH4_1, DH4_0):
            block = int(task == DH4_1)
            if block:
                wait_weights(1, names.theta_b, names.theta_f)
            else:
                wait_weights(0, names.theta_f)
            pp, w = blocks[block].pp, weights[block]
            inward(block, 4, nn(w.theta_b[...], pp[0:512, :]) + nn(w.theta_f[...], pp[512:1024, :]))
        elif task in (B3_1, B2_1, B1_1, B3_0, B2_0, B1_0):
            block = int(task < GB_0)
            depth = 4 - (task - (B3_1 if block else B3_0))
            b, w = blocks[block], weights[block]
            dz = b.d[depth - 1][...]
            store_with_bias(block, (M0, M1, M2)[depth - 2], nt(b.h[depth - 1][...], dz), depth - 1)
            inward(block, depth - 1, nn(w[names.mid0 + depth - 2][...], dz))
        elif task in (B0_1, B0_0):
            block = int(task == B0_1)
            b = blocks[block]
            dz = b.d[0][...]
            store_with_bias(block, FIRST, nt(b.h[0][...], dz), 0)
            number, first = place_of(block, FIRST)
            rounds[number].part[first + 336 : first + 352, :] = b.bias[...].astype(BF16)
            direct = b.gb[...].astype(F32)
            din = (nn(weights[block].first[...], dz) - direct) * s.mask[...].astype(F32)
            if block:
                one.gb[...] = -(din.astype(BF16))
            else:
                s.dinput[...] = din.astype(BF16)
                hand_over(2)
        elif task == GB_0:
            gb = one.gb[...]
            row_sums(0, 6, gb.astype(F32))
            store(0, BACK, nt(gb, one.pp[0:512, :]))
            one.pp[0:512, :] = tn(weights[0].back[...], gb).astype(BF16)
        elif task == GTB_0:
            store_with_bias(0, TB, nt(one.h[4][...], one.pp[0:512, :]), 4)
        elif task == HEADS_0:
            wait_weights(0, names.theta_f)
            theta_f = theta(0, 1)
            store(0, FORE, nt(theta_f, s.gh[...]))
            s.sent[...] = heads(0, theta_f).astype(BF16)
            hand_over(0)
        elif task == THETA_1:
            wait_weights(1, names.theta_b, names.theta_f)
            end_biases(1)
            for k in range(2):
                s.tt[512 * k : 512 * (k + 1), :] = theta(1, k)
            store(1, BACK, nt(two.gb[...], s.tt[0:512, :]))
            store(1, FORE, nt(s.tt[512:1024, :], s.gh[...]))
        else:
            s.total[...] = (s.sent[...].astype(F32) + heads(1, s.tt[512:1024, :])).astype(BF16)
            hand_over(1)
            s.r2[...] = residual(1, s.tt[0:512, :]).astype(BF16)
            hand_over(3)

    def fetch(*keys):
        for block in range(2):

            @pl.when(c == block)
            def _(block=block):
                for key in keys:
                    weight_local(block, key).start()

    def send_weights(*keys):
        for block in range(2):

            @pl.when(c == block)
            def _(block=block):
                for key in keys:
                    weight_remote(block, key).start()

    barrier = pltpu.get_barrier_semaphore()
    greeted = [(other, dp, y)]
    if whole:
        greeted += [
            (c, dp1, rep1),
            (other, dp1, rep1),
            (c, dp2, rep2),
            (other, dp2, rep2),
            (c, dpz, y),
            (c, dpm, y),
        ]
    for device in greeted:
        pl.semaphore_signal(barrier, inc=1, device_id=device, device_id_type=MESH)
    loads.look.start()
    loads.past.start()
    fetch(names.first, names.hid)
    pl.semaphore_wait(barrier, len(greeted))
    send_weights(names.first, names.hid, names.mid0)
    fetch(names.mid0, names.mid1, names.mid2)
    after = {
        LOAD: ((names.fore,), (names.mid1,)),
        Z1_0: ((names.theta_b, names.back, names.backb), (names.mid2, names.fore)),
        Z2_0: ((names.theta_f, names.foreb), (names.theta_b, names.back, names.backb)),
        Z3_0: ((), (names.theta_f, names.foreb)),
    }

    sent = set()
    for item in ORDER:
        if item < STEP:
            run(item)
            if item in after:
                fetch(*after[item][0])
                send_weights(*after[item][1])
            if item == LOAD:
                for load in (loads.label, loads.scored, loads.adjp, loads.adjl):
                    load.start()
            for number in range(len(ROUNDS)):
                if not missing[number] and number not in sent:
                    sent.add(number)
                    message(number, D2D).start()
        elif whole:
            step((item - STEP) // 10, (item - STEP) % 10)
    if not whole:
        for number in range(len(ROUNDS)):
            chip_step(number)

    wait_sends()
    for key in range(11):
        for block in range(2):
            pl.when(c == block)(lambda block=block, key=key: weight_remote(block, key).wait_send())
    handed_over()
    for number, (block, _) in enumerate(ROUNDS):

        @pl.when(c == block)
        def _(number=number):
            for copy in deliver(number):
                copy.wait()


class Final(NamedTuple):
    pair: Any
    outcome: Any
    first: Any
    mid: Any
    theta: Any
    back: Any
    fore: Any
    hid: Any
    backb: Any
    foreb: Any


def widen(treedef, *refs):
    held, outs, near, wide, in_sem, out_sem = jax.tree.unflatten(treedef, refs)
    arriving = [pltpu.make_async_copy(src, dst, in_sem.at[i]) for i, (src, dst) in enumerate(zip(held, near))]
    leaving = [pltpu.make_async_copy(src, dst, out_sem.at[i]) for i, (src, dst) in enumerate(zip(wide, outs))]
    for copy in arriving:
        copy.start()
    for i, copy in enumerate(arriving):
        copy.wait()
        ref = near[i]
        if i == 2:
            wide.first[...] = ref[0:336, :].astype(F32)
            lines = ref[336:352, :].astype(F32)
            for k in range(24):
                at = k % 4 * 128
                wide.hid[k : k + 1, :] = lines[k // 4 : k // 4 + 1, at : at + 128]
            wide.backb[...] = lines[6:7, 0:336]
            wide.foreb[...] = lines[7:8, 0:256]
            for k in (7, 8, 9):
                leaving[k].start()
        else:
            wide[i][...] = ref[...].astype(F32)
        leaving[i].start()
    for copy in leaving:
        copy.wait()


def shards(whole, past, label, look, scored, adjp, adjl, first, mid, theta, back, fore, hid, backb, foreb):
    windows = past.shape[0]
    n = windows // 2
    hbm = pl.BlockSpec(memory_space=pl.ANY)
    shape = jax.ShapeDtypeStruct
    inputs = Inputs(past.T, look.T, label.reshape(windows // 128, 128), scored.T, adjp.T, adjl.T)
    given = Given(first, mid, theta, back[0].T, fore, hid.reshape(24, 128), backb, foreb)
    shapes = Results(
        (64, windows), (336, windows), (352, 512), (3, 512, 512), (2, 512, 512), (336, 512), (512, 256)
    )
    results = Results(*(shape(dims, BF16) for dims in shapes))
    buffers, structure = jax.tree.flatten(scratch(n))
    treedef = jax.tree.structure((inputs, given, results, scratch(n)))
    results = pl.pallas_call(
        functools.partial(body, n, whole, treedef),
        out_shape=results,
        in_specs=[hbm] * 14,
        out_specs=Results(*[hbm] * 7),
        scratch_shapes=buffers,
        compiler_params=pltpu.CompilerParams(
            collective_id=0, has_side_effects=True, vmem_limit_bytes=63 * 2**20
        ),
    )(*inputs, *given)

    shapes = Final(shapes.pair, shapes.outcome, (336, 512), *shapes[3:], (24, 128), (1, 336), (1, 256))
    final = Final(*(shape(dims, F32) for dims in shapes))
    near = Results(*(pltpu.VMEM(held.shape, BF16) for held in results))
    wide = Final(*(pltpu.VMEM(dims, F32) for dims in shapes))
    sems = (pltpu.SemaphoreType.DMA((7,)), pltpu.SemaphoreType.DMA((10,)))
    treedef = jax.tree.structure((results, final, near, wide, *sems))
    final = pl.pallas_call(
        functools.partial(widen, treedef),
        out_shape=final,
        in_specs=[hbm] * 7,
        out_specs=Final(*[hbm] * 10),
        scratch_shapes=[*near, *wide, *sems],
        compiler_params=pltpu.CompilerParams(vmem_limit_bytes=63 * 2**20),
    )(*results)
    if not whole:
        final = Final(*final[:2], *lax.psum(tuple(final[2:]), ("dp", "rep")))
    return (
        final.pair.T[None],
        final.outcome.T[None],
        final.first[None],
        final.mid[None],
        final.theta[None],
        final.back.T[None],
        final.fore[None],
        final.hid.reshape(1, 6, 512),
        final.backb,
        final.foreb,
    )


def solution(mesh):
    wide = P(("dp", "rep"), None)
    s2, s3, s4 = (P("section", *([None] * k)) for k in (1, 2, 3))
    in_specs = (wide, P(("dp", "rep")), wide, wide, wide, wide, s3, s4, s4, s3, s3, s3, s2, s2)
    rowwise = P("section", ("dp", "rep"), None)
    out_specs = (rowwise, rowwise, s3, s4, s4, s3, s3, s3, s2, s2)
    whole = (mesh.shape["dp"], mesh.shape["rep"]) == (8, 2)
    run = functools.partial(shards, whole)
    return jax.shard_map(run, mesh=mesh, in_specs=in_specs, out_specs=out_specs, check_vma=False)
```

```python
import functools
from typing import Any, NamedTuple

import jax
import jax.numpy as jnp
from jax import lax
from jax.experimental import pallas as pl
from jax.experimental.pallas import tpu as pltpu
from jax.sharding import PartitionSpec as P

BF16 = jnp.bfloat16
F32 = jnp.float32
MESH = pl.DeviceIdType.MESH

BACK, FORE, TB, TF, M0, M1, M2, FIRST = range(8)
PIECE_ROWS = (384, 256, 512, 512, 512, 512, 512, 384)
ROUNDS = (
    (0, (TF,)),
    (1, (TB, TF,)),
    (1, (M2, M1,)),
    (1, (M0, FIRST,)),
    (1, (BACK, FORE,)),
    (0, (BACK, FORE, TB,)),
    (0, (M2,)),
    (0, (M1,)),
    (0, (M0,)),
    (0, (FIRST,)),
)
D2D, S1, S2, S3, S4, G3, G2, G1, G1X, GD = range(10)
X, Y, Z, FAR = range(4)
ROUTES = (
    ((Z, X, Y), (X, Y, Z), 3),
    ((X, Y, Z), (Y, X, Z), 3),
    ((Y, X, Z), (Z, Y, X), 3),
    ((Z, Y, X), (Z, X, Y), 3),
    ((Y, X, Z), (X, Y, Z), 3),
    ((Y, X, Z), (Z, Y, X), 3),
    ((Z, X, Y), (X, Y, Z), 3),
    ((Z, X, Y), (X, Y, Z), 3),
    ((Y, X, Z), (X, Y, Z), 3),
    ((Y, X, Z), (X, Y, Z), 2),
)
(
    LOAD, Z1_0, Z2_0, Z3_0, Z4_0, GH_0, GTF_0, BACK_0, Z1_1, Z2_1, Z3_1, Z4_1, PP_1, GT_1, DH4_1,
    B3_1, B2_1, B1_1, B0_1, GB_0, GTB_0, DH4_0, B3_0, B2_0, B1_0, B0_0, HEADS_0, THETA_1, FINAL_1,
) = range(29)
STEP = 1000
ORDER = (
    LOAD, Z1_0, Z2_0, Z3_0, GH_0, Z4_0, BACK_0, Z1_1, Z2_1, Z3_1, PP_1, Z4_1, GT_1, DH4_1, B3_1, 1010, B2_1,
    GTF_0, B1_1, 1020, 1000, B0_1, 1011, GB_0, GTB_0, 1030, THETA_1, 1021, HEADS_0, 1001, 1040, 1012, DH4_0,
    1050, B3_0, 1022, 1002, 1031, B2_0, 1060, 1013, 1041, FINAL_1, 1070, B1_0, 1051, 1003, 1023, 1032, 1061,
    B0_0, 1042, 1080, 1014, 1071, 1090, 1052, 1033, 1004, 1062, 1043, 1081, 1072, 1015, 1024, 1091, 1053,
    1005, 1063, 1082, 1034, 1073, 1016, 1025, 1044, 1092, 1006, 1035, 1083, 1054, 1045, 1064, 1093, 1017,
    1074, 1026, 1007, 1084, 1065, 1036, 1075, 1055, 1046, 1094, 1027, 1066, 1085, 1076, 1056, 1047, 1096,
    1037, 1086, 1067, 1077, 1097, 1057, 1087,
)


def rows_of(number):
    return sum(PIECE_ROWS[piece] for piece in ROUNDS[number][1])


def place_of(block, piece):
    for number, (at, pieces) in enumerate(ROUNDS):
        if at == block and piece in pieces:
            return number, sum(PIECE_ROWS[p] for p in pieces[: pieces.index(piece)])


def rounds_of(block):
    return [number for number, (at, _) in enumerate(ROUNDS) if at == block]


def parts_of(block):
    parts = []
    for number, (at, pieces) in enumerate(ROUNDS):
        first = 0
        half = rows_of(number) // 2
        for piece in pieces if at == block else ():
            count = (336, 256, 512, 512, 512, 512, 512, 352)[piece]
            for core in range(2):
                low, high = max(first, core * half), min(first + count, (core + 1) * half)
                if low < high:
                    parts += [(number, core, low - core * half, high - low, piece, low - first)] * (1 + (piece == FORE))
            first += PIECE_ROWS[piece]
    return parts


def nn(a, b):
    return jnp.dot(a, b, preferred_element_type=F32)


def nt(a, b):
    return lax.dot_general(a, b, (((1,), (1,)), ((), ())), preferred_element_type=F32)


def tn(a, b):
    return lax.dot_general(a, b, (((0,), (0,)), ((), ())), preferred_element_type=F32)


class Inputs(NamedTuple):
    past: Any
    look: Any
    label: Any
    scored: Any
    adjp: Any
    adjl: Any


class Given(NamedTuple):
    first: Any
    mid: Any
    theta: Any
    back: Any
    fore: Any
    hid: Any
    backb: Any
    foreb: Any


class Gathered(NamedTuple):
    own: Any
    rest: Any


class Results(NamedTuple):
    pair: Any
    outcome: Any
    rounds: Any


class Weights(NamedTuple):
    first: Any
    hid: Any
    mid0: Any
    mid1: Any
    mid2: Any
    theta: Any
    back: Any
    backb: Any
    fore: Any
    foreb: Any


class Block(NamedTuple):
    h: Any
    d: Any
    gb: Any
    pp: Any
    bias: Any
    hid: Any
    backb: Any
    foreb: Any


class Round(NamedTuple):
    part: Any
    landing: Any


class Scratch(NamedTuple):
    weights: Any
    blocks: Any
    rounds: Any
    observed: Any
    mask: Any
    label: Any
    scored: Any
    adjp: Any
    gh: Any
    tt: Any
    sent: Any
    total: Any
    dinput: Any
    r2: Any
    load_sem: Any
    weight_sem: Any
    weight_send: Any
    send_sem: Any
    recv_sem: Any
    last_send: Any
    last_recv: Any
    give_send: Any
    give_recv: Any


def scratch(n):
    def weights():
        square = pltpu.VMEM((512, 512), BF16)
        return Weights(
            first=pltpu.VMEM((336, 512), BF16),
            hid=pltpu.VMEM((24, 128), F32),
            mid0=square,
            mid1=square,
            mid2=square,
            theta=pltpu.VMEM((2, 512, 512), BF16),
            back=pltpu.VMEM((336, 512), BF16),
            backb=pltpu.VMEM((1, 336), F32),
            fore=pltpu.VMEM((512, 256), BF16),
            foreb=pltpu.VMEM((1, 256), F32),
        )

    def block():
        return Block(
            h=[pltpu.VMEM(((336 if k == 0 else 512) + 16, n), BF16) for k in range(5)],
            d=[pltpu.VMEM((512, n), BF16) for _ in range(4)],
            gb=pltpu.VMEM((336, n), BF16),
            pp=pltpu.VMEM((1024, n), BF16),
            bias=pltpu.VMEM((16, 512), F32),
            hid=pltpu.VMEM((512, 8), F32),
            backb=pltpu.VMEM((336, 8), F32),
            foreb=pltpu.VMEM((256, 8), F32),
        )

    def a_round(number):
        rows = rows_of(number)
        half = rows // 2

        shapes = [(half, 512)]
        for _ in range(ROUTES[number][2]):
            tall, wide = shapes[-1]
            shapes.append((tall // 2, wide) if tall // 2 % 16 == 0 else (tall, wide // 2))
        shapes += [shapes[-1]] * (5 - len(shapes))
        return Round(
            part=pltpu.VMEM((rows, 512), BF16),
            landing=[pltpu.VMEM(shape, BF16) for shape in shapes[1:]],
        )

    dma = pltpu.SemaphoreType.DMA
    count = len(ROUNDS)
    most = max(len(rounds_of(0)), len(rounds_of(1)))
    return Scratch(
        weights=[weights(), weights()],
        blocks=[block(), block()],
        rounds=[a_round(number) for number in range(count)],
        observed=pltpu.VMEM((336, n), jnp.int32),
        mask=pltpu.VMEM((336, n), BF16),
        label=pltpu.VMEM((n // 128, 128), jnp.int32),
        scored=pltpu.VMEM((64, n), jnp.int32),
        adjp=pltpu.VMEM((64, n), BF16),
        gh=pltpu.VMEM((256, n), BF16),
        tt=pltpu.VMEM((1024, n), BF16),
        sent=pltpu.VMEM((64, n), BF16),
        total=pltpu.VMEM((64, n), BF16),
        dinput=pltpu.VMEM((336, n), BF16),
        r2=pltpu.VMEM((336, n), BF16),
        load_sem=dma((6,)),
        weight_sem=dma((2, 10)),
        weight_send=dma((10,)),
        send_sem=dma((count,)),
        recv_sem=dma((count, 5)),
        last_send=dma((most,)),
        last_recv=dma((most, 2)),
        give_send=dma((4,)),
        give_recv=dma((4,)),
    )


def body(n, whole, treedef, *refs):
    inputs, given, outs, s = jax.tree.unflatten(treedef, refs)
    weights, blocks = s.weights, s.blocks
    rounds = [Round(r.part, [place.own, *r.landing]) for r, place in zip(s.rounds, outs.rounds)]

    c = lax.axis_index("section")
    dp = lax.axis_index("dp")
    y = lax.axis_index("rep")
    z = lax.div(dp, 2)
    x = lax.rem(dp, 2)
    other = 1 - c
    dpx = dp + 1 - 2 * x
    dpz = dp + 2 - 4 * lax.rem(z, 2)
    dpm = 2 * (3 - z) + x
    ry = 1 - y
    chips = ((dpx, y), (dp, ry), (dpz, y), (dpm, y))
    sides = (x, y, lax.rem(lax.div(z + 1, 2), 2))

    def by_core(pair):
        return pair[0] if pair[0] is pair[1] else jnp.where(c == 0, *pair)

    def chip(number, stage):
        if stage == 3:
            return chips[FAR]
        axes = [ROUTES[number][core][stage] for core in range(2)]
        return tuple(by_core([chips[axis][i] for axis in axes]) for i in range(2))

    def side(number, stage, flip=False):
        axes = [ROUTES[number][core ^ flip][stage] for core in range(2)]
        return by_core([sides[axis] for axis in axes])

    mine = pl.ds(pl.multiple_of(c * n, 128), n)
    label_rows = n // 128
    loads = Inputs(
        past=(inputs.past.at[:, mine], blocks[0].h[0].at[pl.ds(0, 336)]),
        look=(inputs.look.at[:, mine], s.observed),
        label=(inputs.label.at[pl.ds(pl.multiple_of(c * label_rows, 8), label_rows)], s.label),
        scored=(inputs.scored.at[:, mine], s.scored),
        adjp=(inputs.adjp.at[:, mine], s.adjp),
        adjl=(inputs.adjl.at[:, mine], blocks[1].gb),
    )
    loads = Inputs(*(pltpu.make_async_copy(*pair, s.load_sem.at[i]) for i, pair in enumerate(loads)))
    sources = Weights(
        first=given.first.at[0],
        hid=given.hid,
        mid0=given.mid.at[0, 0],
        mid1=given.mid.at[0, 1],
        mid2=given.mid.at[0, 2],
        theta=given.theta.at[0],
        back=given.back,
        backb=given.backb,
        fore=given.fore.at[0],
        foreb=given.foreb,
    )

    def weight_local(block, i):
        return pltpu.make_async_copy(sources[i], weights[block][i], s.weight_sem.at[block, i])

    def weight_remote(block, i):
        return pltpu.make_async_remote_copy(
            sources[i],
            weights[block][i],
            s.weight_send.at[i],
            s.weight_sem.at[block, i],
            device_id=(other, dp, y),
            device_id_type=MESH,
        )

    names = Weights(*range(10))

    waited = set()

    def wait_weights(block, *keys):
        for key in keys:
            if (block, key) not in waited:
                waited.add((block, key))
                weight_local(block, key).wait()

    def regions(number, base):
        keep, give = [(base, rows_of(number) // 2, 0, 512)], [None]
        for stage in range(ROUTES[number][2]):
            row, rows, col, cols = keep[-1]
            bit = side(number, stage)
            if rows // 2 % 16 == 0:
                rows = rows // 2
                keep.append((row + bit * rows, rows, col, cols))
                give.append((row + (1 - bit) * rows, rows, col, cols))
            else:
                cols = cols // 2
                keep.append((row, rows, col + bit * cols, cols))
                give.append((row, rows, col + (1 - bit) * cols, cols))

        def at(row, rows, col, cols):
            across = slice(None) if cols == 512 else pl.ds(pl.multiple_of(col, 128), cols)
            return (pl.ds(pl.multiple_of(row, 16), rows), across)

        return [at(*area) for area in keep], [area and at(*area) for area in give]

    def summed(number):
        return regions(number, c * (rows_of(number) // 2))

    def message(number, kind):
        r = rounds[number]
        halvings = ROUTES[number][2]
        half = rows_of(number) // 2
        if kind == D2D:
            where = (pl.ds(pl.multiple_of(other * half, 16), half), slice(None))
            src, dst, device = r.part.at[where], r.landing[D2D], (other, dp, y)
        elif kind <= S4:
            keep, give = summed(number)
            src, dst = r.part.at[give[kind] if kind <= halvings else keep[-1]], r.landing[kind]
            device = (c, *chip(number, kind - S1))
        else:
            stage = {G3: 2, G2: 1, G1: 0, G1X: 0, GD: 0}[kind]
            where = regions(number, 0)[0][stage + 1 if whole else 0]
            src = r.landing[D2D].at[where]
            dst = src if kind <= G1 else outs.rounds[number].rest.at[where]
            device = (other, dp, y) if kind == GD else (other if kind == G1X else c, *chip(number, stage))
        return pltpu.make_async_remote_copy(
            src, dst, *semaphores(number, kind), device_id=device, device_id_type=MESH
        )

    def semaphores(number, kind):
        place = rounds_of(ROUNDS[number][0]).index(number)
        send = s.last_send.at[place] if kind == GD else s.send_sem.at[number]
        if kind >= G1X:
            return send, s.last_recv.at[place, kind - G1X]
        return send, s.recv_sem.at[number, {G1: D2D, G2: S1, G3: S2}.get(kind, kind)]

    latest = {}

    def begin(number, kind):
        if number in latest:
            message(number, latest[number]).wait_send()
        latest[number] = kind
        message(number, kind).start()

    def fold(number, kind, where, *buffer):
        part = rounds[number].part
        part[where] = part[where] + rounds[number].landing[kind][buffer]

    def fold_and_send(number, kind):
        keep, give = summed(number)
        level = kind + 1
        bit = side(number, kind)
        rows, cols = rounds[number].landing[kind].shape

        def of_landing(bit):
            if rows // 2 % 16 == 0:
                return (pl.ds(pl.multiple_of(bit * (rows // 2), 16), rows // 2), slice(None))
            return (slice(None), pl.ds(pl.multiple_of(bit * (cols // 2), 128), cols // 2))

        fold(number, kind, give[level], *of_landing(1 - bit))
        begin(number, level)
        fold(number, kind, keep[level], *of_landing(bit))

    def settle(number, kind):
        r = rounds[number]
        here = regions(number, 0)[0][-1]
        r.landing[D2D][here] = r.part[summed(number)[0][-1]] + r.landing[kind][...]

    def chip_step(number):
        block = ROUNDS[number][0]
        message(number, D2D).wait_recv()
        settle_half(number)
        finish(number)

        pl.when(c == block)(lambda: message(number, GD).wait_recv())

    def settle_half(number):
        r = rounds[number]
        r.landing[D2D][...] = r.landing[D2D][...] + r.part[summed(number)[0][0]]

    def finish(number):
        block = ROUNDS[number][0]
        message(number, latest.pop(number)).wait_send()
        if whole:
            pl.when(c == block)(lambda: message(number, G1).start())
            pl.when(c != block)(lambda: message(number, G1X).start())
        pl.when(c != block)(lambda: message(number, GD).start())

    def step(number, kind):
        block = ROUNDS[number][0]
        halvings = ROUTES[number][2]
        if kind < G1:
            message(number, kind).wait_recv()
        if kind < halvings:
            fold_and_send(number, kind)
        elif kind < S4:
            if kind > halvings:
                message(number, latest.pop(number)).wait_send()
            fold(number, kind, summed(number)[0][-1], ...)
            begin(number, kind + 1)
        elif kind < G1:
            if kind == S4:
                settle(number, kind)
            following = G1 + 1 - halvings if kind == S4 else kind + 1
            if following < G1:
                begin(number, following)
            else:
                finish(number)
        else:

            @pl.when(c == block)
            def _():
                quarter = rows_of(number) // 4
                theirs = side(number, 0, flip=True)
                for kind, ref, at in (
                    (G1, rounds[number].landing[D2D], 1 - side(number, 0)),
                    (GD, outs.rounds[number].rest, theirs),
                    (G1X, outs.rounds[number].rest, 1 - theirs),
                ):
                    ref = ref.at[pl.ds(pl.multiple_of(at * quarter, 16), quarter)]
                    pltpu.make_async_remote_copy(
                        ref, ref, *semaphores(number, kind), device_id=(other, dp, y), device_id_type=MESH
                    ).wait_recv()

    def wait_sends():
        for number, (block, _) in enumerate(ROUNDS):
            if whole:
                pl.when(c == block)(lambda number=number: message(number, G1).wait_send())
                pl.when(c != block)(lambda number=number: message(number, G1X).wait_send())
            pl.when(c != block)(lambda number=number: message(number, GD).wait_send())

    def result(i):
        src = (s.sent, s.total, s.dinput, s.r2)[i]
        dst = (outs.pair, outs.outcome)[i // 2].at[:, mine]
        local = pltpu.make_async_copy(src, dst, s.give_send.at[i])
        remote = pltpu.make_async_remote_copy(
            src, dst, s.give_send.at[i], s.give_recv.at[i], device_id=(other, dp, y), device_id_type=MESH
        )
        return i % 2, local, remote

    def hand_over(i):
        keeper, local, remote = result(i)
        pl.when(c == keeper)(lambda: local.start())
        pl.when(c != keeper)(lambda: remote.start())

    def handed_over():
        for i in range(4):
            keeper, local, remote = result(i)

            @pl.when(c == keeper)
            def _(local=local, remote=remote):
                local.wait()
                remote.wait_recv()

            pl.when(c != keeper)(lambda remote=remote: remote.wait_send())

    missing = [set(pieces) for _, pieces in ROUNDS]

    def store(block, piece, value):
        number, first = place_of(block, piece)
        missing[number].discard(piece)
        value = value.astype(BF16)
        part = rounds[number].part
        if piece == FORE:
            for k in range(2):
                part[first : first + 256, 256 * k : 256 * (k + 1)] = value[256 * k : 256 * (k + 1)]
        else:
            part[first : first + value.shape[0], :] = value

    def store_with_bias(block, piece, value, row):
        k = value.shape[0] - 16
        blocks[block].bias[row : row + 1, :] = value[k : k + 1]
        store(block, piece, value[:k])

    def row_sums(block, row, value):
        folded = value[:, 0:128]
        for i in range(1, n // 128):
            folded = folded + value[:, 128 * i : 128 * (i + 1)]
        sums = nt(jnp.ones((16, 128), BF16), folded.astype(BF16))
        blocks[block].bias[row : row + 1, 0 : value.shape[0]] = sums[0:1]

    def layer(block, depth):
        b, w = blocks[block], weights[block]
        h = b.h[depth - 1]
        zed = tn(w[(names.first, names.mid0, names.mid1, names.mid2)[depth - 1]][...], h[0 : h.shape[0] - 16, :])
        zed = zed + b.hid[:, depth - 1 : depth]
        sig = 0.5 * jnp.tanh(0.5 * zed) + 0.5
        out = zed * sig
        b.h[depth][0:512, :] = out.astype(BF16)
        b.d[depth - 1][...] = (sig + out * (1.0 - sig)).astype(BF16)

    def theta(block, k):
        return (tn(weights[block].theta[k], blocks[block].h[4][0:512, :]) + blocks[block].hid[:, 4 + k : 5 + k]).astype(BF16)

    def heads(block, theta_f):
        wide = tn(weights[block].fore[...], theta_f) + blocks[block].foreb[:, 0:1]
        row = label_row()
        chosen = jnp.zeros((64, n), F32)
        for g in range(4):
            chosen = chosen + jnp.where(row == g, wide[64 * g : 64 * (g + 1)], 0.0)
        return chosen * s.scored[...].astype(F32)

    def residual(block, theta_b):
        backcast = nn(weights[block].back[...], theta_b) + blocks[block].backb[:, 0:1]
        return (blocks[block].h[0][0:336, :].astype(F32) - backcast) * s.mask[...].astype(F32)

    def inward(block, depth, dh):
        d = blocks[block].d[depth - 1]
        d[...] = (dh * d[...].astype(F32)).astype(BF16)

    def layer_biases(block):
        b, w = blocks[block], weights[block]
        lines = [
            jnp.concatenate([w.hid[4 * k + i : 4 * k + i + 1, :] for i in range(4)], axis=1) for k in range(6)
        ]
        lines.append(jnp.zeros((2, 512), F32))
        b.hid[...] = jnp.concatenate(lines, axis=0).T

    def end_biases(block):
        b, w = blocks[block], weights[block]
        b.backb[...] = jnp.broadcast_to(w.backb[...], (8, 336)).T
        b.foreb[...] = jnp.broadcast_to(w.foreb[...], (8, 256)).T

    def label_row():
        return jnp.concatenate([s.label[i : i + 1, :] for i in range(label_rows)], axis=1)

    def run(task):
        one, two = blocks
        if task == LOAD:
            loads.look.wait()
            mask = s.observed[...].astype(F32).astype(BF16)
            s.mask[...] = mask
            loads.past.wait()
            one.h[0][0:336, :] = one.h[0][0:336, :] * mask
            wait_weights(0, names.hid)
            layer_biases(0)
        elif task in (Z1_0, Z2_0, Z3_0, Z4_0):
            depth = task - Z1_0 + 1
            if depth == 1:
                wait_weights(0, names.first, names.mid0)
            elif depth == 3:
                wait_weights(0, names.mid1, names.mid2)
            layer(0, depth)
        elif task in (Z1_1, Z2_1, Z3_1, Z4_1):
            depth = task - Z1_1 + 1
            if depth == 1:
                wait_weights(1, *range(10))
                layer_biases(1)
            layer(1, depth)
        elif task == GH_0:
            wait_weights(0, *late)
            for load in (loads.label, loads.scored, loads.adjp, loads.adjl):
                load.wait()
            for b in blocks:
                for h in b.h:
                    k = h.shape[0] - 16
                    h[k : k + 16, :] = jnp.ones((16, n), BF16)
                b.bias[...] = jnp.zeros((16, 512), F32)
            df = s.adjp[...].astype(F32) * s.scored[...].astype(F32)
            row = label_row()
            gh = jnp.concatenate([jnp.where(row == g, df, 0.0) for g in range(4)], axis=0)
            s.gh[...] = gh.astype(BF16)
            for block in range(2):
                row_sums(block, 7, gh)
            one.pp[512:1024, :] = nn(weights[0].fore[...], s.gh[...]).astype(BF16)
        elif task == GTF_0:
            store_with_bias(0, TF, nt(one.h[4][...], one.pp[512:1024, :]), 5)
        elif task == BACK_0:
            end_biases(0)
            theta_b = theta(0, 0)
            one.pp[0:512, :] = theta_b
            two.h[0][0:336, :] = residual(0, theta_b).astype(BF16)
        elif task == PP_1:
            gb = -(two.gb[...] * s.mask[...])
            two.gb[...] = gb
            row_sums(1, 6, gb.astype(F32))
            two.pp[0:512, :] = tn(weights[1].back[...], gb).astype(BF16)
            two.pp[512:1024, :] = nn(weights[1].fore[...], s.gh[...]).astype(BF16)
        elif task == GT_1:
            for k in range(2):
                store_with_bias(1, (TB, TF)[k], nt(two.h[4][...], two.pp[512 * k : 512 * (k + 1), :]), 4 + k)
        elif task in (DH4_1, DH4_0):
            block = int(task == DH4_1)
            pp, w = blocks[block].pp, weights[block]
            inward(block, 4, nn(w.theta[0], pp[0:512, :]) + nn(w.theta[1], pp[512:1024, :]))
        elif task in (B3_1, B2_1, B1_1, B3_0, B2_0, B1_0):
            block = int(task < GB_0)
            depth = 4 - (task - (B3_1 if block else B3_0))
            b, w = blocks[block], weights[block]
            dz = b.d[depth - 1][...]
            store_with_bias(block, (M0, M1, M2)[depth - 2], nt(b.h[depth - 1][...], dz), depth - 1)
            inward(block, depth - 1, nn(w[names.mid0 + depth - 2][...], dz))
        elif task in (B0_1, B0_0):
            block = int(task == B0_1)
            b = blocks[block]
            dz = b.d[0][...]
            store_with_bias(block, FIRST, nt(b.h[0][...], dz), 0)
            number, first = place_of(block, FIRST)
            rounds[number].part[first + 336 : first + 352, :] = b.bias[...].astype(BF16)
            direct = b.gb[...].astype(F32)
            din = (nn(weights[block].first[...], dz) - direct) * s.mask[...].astype(F32)
            if block:
                one.gb[...] = -(din.astype(BF16))
            else:
                s.dinput[...] = din.astype(BF16)
                hand_over(2)
        elif task == GB_0:
            gb = one.gb[...]
            row_sums(0, 6, gb.astype(F32))
            store(0, BACK, nt(gb, one.pp[0:512, :]))
            one.pp[0:512, :] = tn(weights[0].back[...], gb).astype(BF16)
        elif task == GTB_0:
            store_with_bias(0, TB, nt(one.h[4][...], one.pp[0:512, :]), 4)
        elif task == HEADS_0:
            theta_f = theta(0, 1)
            store(0, FORE, nt(theta_f, s.gh[...]))
            s.sent[...] = heads(0, theta_f).astype(BF16)
            hand_over(0)
        elif task == THETA_1:
            end_biases(1)
            for k in range(2):
                s.tt[512 * k : 512 * (k + 1), :] = theta(1, k)
            store(1, BACK, nt(two.gb[...], s.tt[0:512, :]))
            store(1, FORE, nt(s.tt[512:1024, :], s.gh[...]))
        else:
            s.total[...] = (s.sent[...].astype(F32) + heads(1, s.tt[512:1024, :])).astype(BF16)
            hand_over(1)
            s.r2[...] = residual(1, s.tt[0:512, :]).astype(BF16)
            hand_over(3)

    def fetch(*keys):
        for block in range(2):

            @pl.when(c == block)
            def _(block=block):
                for key in keys:
                    weight_local(block, key).start()

    def send_weights(*keys):
        for block in range(2):

            @pl.when(c == block)
            def _(block=block):
                for key in keys:
                    weight_remote(block, key).start()

    barrier = pltpu.get_barrier_semaphore()
    greeted = [(other, dp, y)]
    if whole:
        greeted += [(c, *place) for place in chips] + [(other, *place) for place in chips[:FAR]]
    for device in greeted:
        pl.semaphore_signal(barrier, inc=1, device_id=device, device_id_type=MESH)
    loads.look.start()
    loads.past.start()
    fetch(names.first, names.hid, names.mid0)
    pl.semaphore_wait(barrier, len(greeted))
    send_weights(names.first, names.hid, names.mid0)
    late = (names.fore, names.theta, names.back, names.backb, names.foreb)
    after = {LOAD: ((names.mid1, names.mid2, *late), (names.mid1, names.mid2)), Z2_0: ((), late)}

    sent = set()
    for item in ORDER:
        if item < STEP:
            run(item)
            if item in after:
                fetch(*after[item][0])
                send_weights(*after[item][1])
            if item == LOAD:
                for load in (loads.label, loads.scored, loads.adjp, loads.adjl):
                    load.start()
            for number in range(len(ROUNDS)):
                if not missing[number] and number not in sent:
                    sent.add(number)
                    begin(number, D2D)
        elif whole:
            step((item - STEP) // 10, (item - STEP) % 10)
    if not whole:
        for number in range(len(ROUNDS)):
            chip_step(number)

    wait_sends()
    for key in range(10):
        for block in range(2):
            pl.when(c == block)(lambda block=block, key=key: weight_remote(block, key).wait_send())
    handed_over()


class Final(NamedTuple):
    pair: Any
    outcome: Any
    first: Any
    mid: Any
    theta: Any
    back: Any
    fore: Any
    hid: Any
    backb: Any
    foreb: Any


def widen(treedef, *refs):
    held, outs, wide, sem = jax.tree.unflatten(treedef, refs)
    names = Final(*range(10))

    def leaving(i):
        return pltpu.make_async_copy(wide[i], outs[i], sem.at[i])

    def take(block):
        parts = parts_of(block)
        for i, part in enumerate(parts):
            number, core, low, count, piece, first = part
            source = held.rounds[number].own if core == block else held.rounds[number].rest
            rows = source[low : low + count, :].astype(F32)
            if piece == FORE:
                k = int(parts[i - 1] == part)
                wide.fore[256 * k + first : 256 * k + first + count, :] = rows[:, 256 * k : 256 * (k + 1)]
            elif piece == FIRST:
                used = min(count, 336 - first)
                wide.first[first : first + used, :] = rows[:used]
                if used < count:
                    lines = rows[used : used + 8]
                    for k in range(24):
                        at = k % 4 * 128
                        wide.hid[k : k + 1, :] = lines[k // 4 : k // 4 + 1, at : at + 128]
                    wide.backb[...] = lines[6:7, 0:336]
                    wide.foreb[...] = lines[7:8, 0:256]
            elif piece == BACK:
                wide.back[first : first + count, :] = rows
            elif piece in (TB, TF):
                wide.theta[piece - TB, first : first + count, :] = rows
            else:
                wide.mid[piece - M0, first : first + count, :] = rows

    wide.outcome[...] = held.outcome[...].astype(F32)
    leaving(names.outcome).start()
    wide.pair[...] = held.pair[...].astype(F32)
    leaving(names.pair).start()
    c = lax.axis_index("section")
    for block in range(2):
        pl.when(c == block)(functools.partial(take, block))
    for i in range(2, 10):
        leaving(i).start()
    for i in range(10):
        leaving(i).wait()


def shards(whole, past, label, look, scored, adjp, adjl, first, mid, theta, back, fore, hid, backb, foreb):
    windows = past.shape[0]
    n = windows // 2
    hbm = pl.BlockSpec(memory_space=pl.ANY)
    shape = jax.ShapeDtypeStruct
    inputs = Inputs(past.T, look.T, label.reshape(windows // 128, 128), scored.T, adjp.T, adjl.T)
    given = Given(first, mid, theta, back[0].T, fore, hid.reshape(24, 128), backb, foreb)
    results = Results(
        pair=pltpu.VMEM((64, windows), BF16),
        outcome=pltpu.VMEM((336, windows), BF16),
        rounds=[
            Gathered(*[pltpu.VMEM((rows_of(number) // 2, 512), BF16)] * 2) for number in range(len(ROUNDS))
        ],
    )
    buffers = jax.tree.leaves(scratch(n))
    treedef = jax.tree.structure((inputs, given, results, scratch(n)))
    near = pl.BlockSpec(memory_space=pltpu.VMEM)
    places = jax.tree.leaves(results)
    held = pl.pallas_call(
        functools.partial(body, n, whole, treedef),
        out_shape=places,
        in_specs=[hbm] * 14,
        out_specs=[near] * len(places),
        scratch_shapes=buffers,
        compiler_params=pltpu.CompilerParams(
            collective_id=0, has_side_effects=True, vmem_limit_bytes=54 * 2**20
        ),
    )(*inputs, *given)

    shapes = Final(
        pair=(64, windows),
        outcome=(336, windows),
        first=(336, 512),
        mid=(3, 512, 512),
        theta=(2, 512, 512),
        back=(336, 512),
        fore=(512, 256),
        hid=(24, 128),
        backb=(1, 336),
        foreb=(1, 256),
    )
    final = Final(*(shape(dims, F32) for dims in shapes))
    wide = Final(*(pltpu.VMEM(dims, F32) for dims in shapes))
    sem = pltpu.SemaphoreType.DMA((10,))
    treedef = jax.tree.structure((results, final, wide, sem))
    final = pl.pallas_call(
        functools.partial(widen, treedef),
        out_shape=final,
        in_specs=[near] * len(places),
        out_specs=Final(*[hbm] * 10),
        scratch_shapes=[*wide, sem],
        compiler_params=pltpu.CompilerParams(vmem_limit_bytes=32 * 2**20),
    )(*held)
    if not whole:
        final = Final(*final[:2], *lax.psum(tuple(final[2:]), ("dp", "rep")))
    return (
        final.pair.T[None],
        final.outcome.T[None],
        final.first[None],
        final.mid[None],
        final.theta[None],
        final.back.T[None],
        final.fore[None],
        final.hid.reshape(1, 6, 512),
        final.backb,
        final.foreb,
    )


def solution(mesh):
    wide = P(("dp", "rep"), None)
    s2, s3, s4 = (P("section", *([None] * k)) for k in (1, 2, 3))
    in_specs = (wide, P(("dp", "rep")), wide, wide, wide, wide, s3, s4, s4, s3, s3, s3, s2, s2)
    rowwise = P("section", ("dp", "rep"), None)
    out_specs = (rowwise, rowwise, s3, s4, s4, s3, s3, s3, s2, s2)
    whole = (mesh.shape["dp"], mesh.shape["rep"]) == (8, 2)
    run = functools.partial(shards, whole)
    return jax.shard_map(run, mesh=mesh, in_specs=in_specs, out_specs=out_specs, check_vma=False)
```

```python
import functools
from typing import Any, NamedTuple

import jax
import jax.numpy as jnp
from jax import lax
from jax.experimental import pallas as pl
from jax.experimental.pallas import tpu as pltpu
from jax.sharding import PartitionSpec as P

BF16 = jnp.bfloat16
F32 = jnp.float32
MESH = pl.DeviceIdType.MESH

BACK, FORE, TB, TF, M0, M1, M2, FIRST = range(8)
PIECE_ROWS = (384, 256, 512, 512, 512, 512, 512, 384)
ROUNDS = (
    (0, (TF,)),
    (1, (TB, TF,)),
    (1, (M2,)),
    (1, (M1,)),
    (1, (M0, FIRST,)),
    (1, (BACK, FORE,)),
    (0, (BACK, FORE, TB,)),
    (0, (M2,)),
    (0, (M1,)),
    (0, (M0,)),
    (0, (FIRST,)),
)
D2D, S1, S2, S3, S4, G3, G2, G1, G1X, GD = range(10)
X, Y, Z, FAR = range(4)
ROUTES = (
    ((X, Z, Y), (Y, X, Z)),
    ((Y, Z, X), (X, Y, Z)),
    ((Y, X, Z), (Y, X, Z)),
    ((X, Z, Y), (Z, Y, X)),
    ((Z, X, Y), (X, Y, Z)),
    ((Z, Y, X), (X, Y, Z)),
    ((Y, X, Z), (Z, Y, X)),
    ((Y, X, Z), (X, Z, Y)),
    ((Z, Y, X), (X, Y, Z)),
    ((X, Y, Z), (Y, X, Z)),
    ((Y, X, Z), (X, Y, Z)),
)
(
    LOAD, Z1_0, Z2_0, Z3_0, Z4_0, GH_0, GTF_0, BACK_0, Z1_1, Z2_1, Z3_1, Z4_1, PP_1, GT_1, DH4_1,
    B3_1, B2_1, B1_1, B0_1, GB_0, GTB_0, DH4_0, B3_0, B2_0, B1_0, B0_0, HEADS_0, THETA_1, FINAL_1, GTF_1,
) = range(30)
STEP = 1000
ORDER = (
    LOAD, Z1_0, Z2_0, Z3_0, Z4_0, BACK_0, Z1_1, GH_0, Z2_1, PP_1, Z3_1, Z4_1, GT_1, GTF_1, DH4_1, B3_1, 1010,
    B2_1, B1_1, B0_1, 1020, 1030, GB_0, 1011, 1040, HEADS_0, GTF_0, GTB_0, 1031, DH4_0, 1000, 1021, 1060,
    1012, THETA_1, 1041, B3_0, 1001, 1050, 1032, 1022, B2_0, 1070, 1061, 1013, B1_0, 1080, 1002, 1042, 1033,
    1051, FINAL_1, 1071, 1023, 1090, B0_0, 1062, 1014, 1081, 1003, 1100, 1052, 1043, 1024, 1091, 1072, 1034,
    1015, 1063, 1082, 1053, 1101, 1004, 1092, 1025, 1073, 1035, 1044, 1016, 1102, 1083, 1005, 1026, 1064,
    1093, 1054, 1036, 1045, 1103, 1074, 1006, 1084, 1065, 1094, 1055, 1104, 1046, 1075, 1085, 1095, 1066,
    1105, 1056, 1086, 1076, 1096, 1106,
)


def rows_of(number):
    return sum(PIECE_ROWS[piece] for piece in ROUNDS[number][1])


def place_of(block, piece):
    for number, (at, pieces) in enumerate(ROUNDS):
        if at == block and piece in pieces:
            return number, sum(PIECE_ROWS[p] for p in pieces[: pieces.index(piece)])


def rounds_of(block):
    return [number for number, (at, _) in enumerate(ROUNDS) if at == block]


def in_line(number, core):
    return ROUTES[number][core][2] == Z


def parts_of(block):
    parts = []
    for number, (at, pieces) in enumerate(ROUNDS):
        first = 0
        half = rows_of(number) // 2
        for piece in pieces if at == block else ():
            count = (336, 256, 512, 512, 512, 512, 512, 352)[piece]
            for core in range(2):
                low, high = max(first, core * half), min(first + count, (core + 1) * half)
                if low < high:
                    parts += [(number, core, low - core * half, high - low, piece, low - first)] * (1 + (piece == FORE))
            first += PIECE_ROWS[piece]
    return parts


def nn(a, b):
    return jnp.dot(a, b, preferred_element_type=F32)


def nt(a, b):
    return lax.dot_general(a, b, (((1,), (1,)), ((), ())), preferred_element_type=F32)


def tn(a, b):
    return lax.dot_general(a, b, (((0,), (0,)), ((), ())), preferred_element_type=F32)


class Inputs(NamedTuple):
    past: Any
    look: Any
    label: Any
    scored: Any
    adjp: Any
    adjl: Any


class Given(NamedTuple):
    first: Any
    mid: Any
    theta: Any
    back: Any
    fore: Any
    hid: Any
    backb: Any
    foreb: Any


class Gathered(NamedTuple):
    own: Any
    rest: Any


class Results(NamedTuple):
    pair: Any
    outcome: Any
    rounds: Any


class Weights(NamedTuple):
    first: Any
    hid: Any
    mid0: Any
    mid1: Any
    mid2: Any
    theta: Any
    back: Any
    backb: Any
    fore: Any
    foreb: Any


class Block(NamedTuple):
    h: Any
    d: Any
    gb: Any
    pp: Any
    bias: Any
    hid: Any
    backb: Any
    foreb: Any


class Round(NamedTuple):
    part: Any
    landing: Any


class Scratch(NamedTuple):
    weights: Any
    blocks: Any
    rounds: Any
    observed: Any
    mask: Any
    label: Any
    scored: Any
    adjp: Any
    gh: Any
    tt: Any
    sent: Any
    total: Any
    dinput: Any
    r2: Any
    load_sem: Any
    weight_sem: Any
    weight_send: Any
    send_sem: Any
    recv_sem: Any
    out_send: Any
    last_send: Any
    last_recv: Any
    give_send: Any
    give_recv: Any


def scratch(n):
    def weights():
        square = pltpu.VMEM((512, 512), BF16)
        return Weights(
            first=pltpu.VMEM((336, 512), BF16),
            hid=pltpu.VMEM((24, 128), F32),
            mid0=square,
            mid1=square,
            mid2=square,
            theta=pltpu.VMEM((2, 512, 512), BF16),
            back=pltpu.VMEM((336, 512), BF16),
            backb=pltpu.VMEM((1, 336), F32),
            fore=pltpu.VMEM((512, 256), BF16),
            foreb=pltpu.VMEM((1, 256), F32),
        )

    def block():
        return Block(
            h=[pltpu.VMEM(((336 if k == 0 else 512) + 16, n), BF16) for k in range(5)],
            d=[pltpu.VMEM((512, n), BF16) for _ in range(4)],
            gb=pltpu.VMEM((336, n), BF16),
            pp=pltpu.VMEM((1024, n), BF16),
            bias=pltpu.VMEM((16, 512), F32),
            hid=pltpu.VMEM((512, 8), F32),
            backb=pltpu.VMEM((336, 8), F32),
            foreb=pltpu.VMEM((256, 8), F32),
        )

    def a_round(number):
        rows = rows_of(number)
        half = rows // 2

        shapes = [(half, 512)]
        for _ in range(3):
            tall, wide = shapes[-1]
            shapes.append((tall // 2, wide) if tall // 2 % 16 == 0 else (tall, wide // 2))
        largest = shapes[2 if in_line(number, 0) or in_line(number, 1) else 3]
        shapes = [*shapes[:3], largest, largest]
        return Round(
            part=pltpu.VMEM((rows, 512), BF16),
            landing=[pltpu.VMEM(shape, BF16) for shape in shapes[1:]],
        )

    dma = pltpu.SemaphoreType.DMA
    count = len(ROUNDS)
    most = max(len(rounds_of(0)), len(rounds_of(1)))
    return Scratch(
        weights=[weights(), weights()],
        blocks=[block(), block()],
        rounds=[a_round(number) for number in range(count)],
        observed=pltpu.VMEM((336, n), jnp.int32),
        mask=pltpu.VMEM((336, n), BF16),
        label=pltpu.VMEM((n // 128, 128), jnp.int32),
        scored=pltpu.VMEM((64, n), jnp.int32),
        adjp=pltpu.VMEM((64, n), BF16),
        gh=pltpu.VMEM((256, n), BF16),
        tt=pltpu.VMEM((1024, n), BF16),
        sent=pltpu.VMEM((64, n), BF16),
        total=pltpu.VMEM((64, n), BF16),
        dinput=pltpu.VMEM((336, n), BF16),
        r2=pltpu.VMEM((336, n), BF16),
        load_sem=dma((6,)),
        weight_sem=dma((2, 10)),
        weight_send=dma((10,)),
        send_sem=dma((count,)),
        recv_sem=dma((count, 5)),
        out_send=dma((count,)),
        last_send=dma((most,)),
        last_recv=dma((most, 2)),
        give_send=dma((4,)),
        give_recv=dma((4,)),
    )


def body(n, whole, treedef, *refs):
    inputs, given, outs, s = jax.tree.unflatten(treedef, refs)
    weights, blocks = s.weights, s.blocks
    rounds = [Round(r.part, [place.own, *r.landing]) for r, place in zip(s.rounds, outs.rounds)]

    c = lax.axis_index("section")
    dp = lax.axis_index("dp")
    y = lax.axis_index("rep")
    z = lax.div(dp, 2)
    x = lax.rem(dp, 2)
    other = 1 - c
    dpx = dp + 1 - 2 * x
    dpz = dp + 2 - 4 * lax.rem(z, 2)
    dpm = 2 * (3 - z) + x
    ry = 1 - y
    chips = ((dpx, y), (dp, ry), (dpz, y), (dpm, y))
    sides = (x, y, lax.rem(lax.div(z + 1, 2), 2))

    between = (z == 1) | (z == 2)
    ends = (z == 0) | (z == 3)

    mine = pl.ds(pl.multiple_of(c * n, 128), n)
    label_rows = n // 128
    loads = Inputs(
        past=(inputs.past.at[:, mine], blocks[0].h[0].at[pl.ds(0, 336)]),
        look=(inputs.look.at[:, mine], s.observed),
        label=(inputs.label.at[pl.ds(pl.multiple_of(c * label_rows, 8), label_rows)], s.label),
        scored=(inputs.scored.at[:, mine], s.scored),
        adjp=(inputs.adjp.at[:, mine], s.adjp),
        adjl=(inputs.adjl.at[:, mine], blocks[1].gb),
    )
    loads = Inputs(*(pltpu.make_async_copy(*pair, s.load_sem.at[i]) for i, pair in enumerate(loads)))
    sources = Weights(
        first=given.first.at[0],
        hid=given.hid,
        mid0=given.mid.at[0, 0],
        mid1=given.mid.at[0, 1],
        mid2=given.mid.at[0, 2],
        theta=given.theta.at[0],
        back=given.back,
        backb=given.backb,
        fore=given.fore.at[0],
        foreb=given.foreb,
    )

    def weight_local(block, i):
        return pltpu.make_async_copy(sources[i], weights[block][i], s.weight_sem.at[block, i])

    def weight_remote(block, i):
        return pltpu.make_async_remote_copy(
            sources[i],
            weights[block][i],
            s.weight_send.at[i],
            s.weight_sem.at[block, i],
            device_id=(other, dp, y),
            device_id_type=MESH,
        )

    names = Weights(*range(10))

    waited = set()

    def wait_weights(block, *keys):
        for key in keys:
            if (block, key) not in waited:
                waited.add((block, key))
                weight_local(block, key).wait()

    def regions(number, core, base):
        keep, give = [(base, rows_of(number) // 2, 0, 512)], [None]
        for axis in ROUTES[number][core]:
            row, rows, col, cols = keep[-1]
            bit = sides[axis]
            if rows // 2 % 16 == 0:
                rows = rows // 2
                keep.append((row + bit * rows, rows, col, cols))
                give.append((row + (1 - bit) * rows, rows, col, cols))
            else:
                cols = cols // 2
                keep.append((row, rows, col + bit * cols, cols))
                give.append((row, rows, col + (1 - bit) * cols, cols))

        def at(row, rows, col, cols):
            across = slice(None) if cols == 512 else pl.ds(pl.multiple_of(col, 128), cols)
            return (pl.ds(pl.multiple_of(row, 16), rows), across)

        return [at(*area) for area in keep], [area and at(*area) for area in give]

    def summed(number, core):
        return regions(number, core, core * (rows_of(number) // 2))

    def gathered(number, core):
        return regions(number, core, 0)[0]

    def landing(number, core, kind):
        ref = rounds[number].landing[kind]
        if kind < S3 or in_line(number, core):
            return ref
        rows, cols = rounds[number].landing[S2].shape
        rows, cols = (rows // 2, cols) if rows // 2 % 16 == 0 else (rows, cols // 2)
        return ref.at[pl.ds(0, rows), pl.ds(0, cols)]

    def message(number, core, kind):
        r = rounds[number]
        half = rows_of(number) // 2
        if kind == D2D:
            where = (pl.ds(pl.multiple_of((1 - core) * half, 16), half), slice(None))
            src, dst, device = r.part.at[where], r.landing[D2D], (1 - core, dp, y)
        elif kind == GD and not whole:
            src, dst, device = r.landing[D2D], outs.rounds[number].rest, (1 - core, dp, y)
        else:
            axes = (*ROUTES[number][core], FAR)
            stage = {G3: 2, G2: 1, G1: 0, G1X: 0, GD: 0}.get(kind, kind - S1)
            last = 2 if in_line(number, core) else 3
            if kind <= S4:
                keep, give = summed(number, core)
                src, dst = r.part.at[give[kind] if kind <= last else keep[last]], landing(number, core, kind)
            else:
                where = gathered(number, core)[min(stage + 1, last)]
                src = r.landing[D2D].at[where]
                dst = src if kind <= G1 else outs.rounds[number].rest.at[where]
            place = (dp, y) if kind == GD else chips[axes[stage]]
            device = (1 - core if kind >= G1X else core, *place)
        return pltpu.make_async_remote_copy(
            src, dst, *semaphores(number, core, kind), device_id=device, device_id_type=MESH
        )

    def semaphores(number, core, kind):
        place = rounds_of(ROUNDS[number][0]).index(number)
        send = s.send_sem.at[number]
        if kind == GD:
            send = s.last_send.at[place]
        elif kind == G3 and whole and in_line(number, core):
            send = s.out_send.at[number]
        if kind >= G1X:
            return send, s.last_recv.at[place, kind - G1X]
        return send, s.recv_sem.at[number, {G1: D2D, G2: S1, G3: S2}.get(kind, kind)]

    def begin(number, core, kind, before):
        message(number, core, before).wait_send()
        message(number, core, kind).start()

    def fold(number, core, kind, where, *buffer):
        part = rounds[number].part
        part[where] = part[where] + landing(number, core, kind)[buffer]

    def fold_and_send(number, core, kind):
        keep, give = summed(number, core)
        level = kind + 1
        bit = sides[ROUTES[number][core][kind]]
        rows, cols = rounds[number].landing[kind].shape

        def of_landing(bit):
            if rows // 2 % 16 == 0:
                return (pl.ds(pl.multiple_of(bit * (rows // 2), 16), rows // 2), slice(None))
            return (slice(None), pl.ds(pl.multiple_of(bit * (cols // 2), 128), cols // 2))

        fold(number, core, kind, give[level], *of_landing(1 - bit))
        begin(number, core, level, kind)
        fold(number, core, kind, keep[level], *of_landing(bit))

    def settle(number, core, level):
        r = rounds[number]
        here = gathered(number, core)[level]
        r.landing[D2D][here] = r.part[summed(number, core)[0][level]] + landing(number, core, S4)[...]

    def chip_step(number, core):
        block = ROUNDS[number][0]
        r = rounds[number]
        half = rows_of(number) // 2
        message(number, core, D2D).wait_recv()
        r.landing[D2D][...] = r.landing[D2D][...] + r.part[core * half : (core + 1) * half, :]
        message(number, core, D2D).wait_send()
        if core == block:
            message(number, 1 - core, GD).wait_recv()
        else:
            message(number, core, GD).start()

    def step(number, core, kind):
        block = ROUNDS[number][0]
        line = in_line(number, core)
        keep2 = summed(number, core)[0][2]
        if line and kind in (S3, S4):

            @pl.when(between)
            def _():
                message(number, core, kind).wait_recv()
                if kind == S3:
                    fold(number, core, S3, keep2, ...)
                    begin(number, core, S4, S2)
                else:
                    settle(number, core, 2)
                    message(number, core, G3).start()
                    begin(number, core, G2, S4)

        elif line and kind == G3:

            @pl.when(ends)
            def _():
                message(number, core, G3).wait_recv()
                begin(number, core, G2, S3)

        else:
            message(number, core, kind).wait_recv()
            if kind == S2 and line:
                fold(number, core, S2, keep2, ...)
                pl.when(ends)(lambda: begin(number, core, S3, S2))
            elif kind < S3:
                fold_and_send(number, core, kind)
            elif kind == S3:
                fold(number, core, kind, summed(number, core)[0][3], ...)
                begin(number, core, S4, S3)
            elif kind == S4:
                settle(number, core, 3)
                begin(number, core, G3, S4)
            elif kind == G3:
                begin(number, core, G2, G3)
            else:
                message(number, core, G2).wait_send()
                if core == block:
                    message(number, core, G1).start()
                else:
                    message(number, core, G1X).start()
                    message(number, core, GD).start()

    def gathered_all(core):
        for number in rounds_of(core) if whole else ():
            quarter = rows_of(number) // 4
            theirs = sides[ROUTES[number][1 - core][0]]
            for kind, ref, at in (
                (G1, rounds[number].landing[D2D], 1 - sides[ROUTES[number][core][0]]),
                (GD, outs.rounds[number].rest, theirs),
                (G1X, outs.rounds[number].rest, 1 - theirs),
            ):
                ref = ref.at[pl.ds(pl.multiple_of(at * quarter, 16), quarter)]
                pltpu.make_async_remote_copy(
                    ref, ref, *semaphores(number, core, kind), device_id=(other, dp, y), device_id_type=MESH
                ).wait_recv()

    def wait_sends(core):
        for number, (block, _) in enumerate(ROUNDS):
            if whole:
                message(number, core, G1 if core == block else G1X).wait_send()
                if in_line(number, core):
                    pl.when(between)(lambda number=number: message(number, core, G3).wait_send())
            if core != block:
                message(number, core, GD).wait_send()

    def on_each_core(do):
        for core in range(2):
            pl.when(c == core)(functools.partial(do, core))

    def result(i):
        src = (s.sent, s.total, s.dinput, s.r2)[i]
        dst = (outs.pair, outs.outcome)[i // 2].at[:, mine]
        local = pltpu.make_async_copy(src, dst, s.give_send.at[i])
        remote = pltpu.make_async_remote_copy(
            src, dst, s.give_send.at[i], s.give_recv.at[i], device_id=(other, dp, y), device_id_type=MESH
        )
        return i % 2, local, remote

    def hand_over(i):
        keeper, local, remote = result(i)
        pl.when(c == keeper)(lambda: local.start())
        pl.when(c != keeper)(lambda: remote.start())

    def handed_over():
        for i in range(4):
            keeper, local, remote = result(i)

            @pl.when(c == keeper)
            def _(local=local, remote=remote):
                local.wait()
                remote.wait_recv()

            pl.when(c != keeper)(lambda remote=remote: remote.wait_send())

    missing = [set(pieces) for _, pieces in ROUNDS]

    def store(block, piece, value):
        number, first = place_of(block, piece)
        missing[number].discard(piece)
        value = value.astype(BF16)
        part = rounds[number].part
        if piece == FORE:
            for k in range(2):
                part[first : first + 256, 256 * k : 256 * (k + 1)] = value[256 * k : 256 * (k + 1)]
        else:
            part[first : first + value.shape[0], :] = value

    def store_with_bias(block, piece, value, row):
        k = value.shape[0] - 16
        blocks[block].bias[row : row + 1, :] = value[k : k + 1]
        store(block, piece, value[:k])

    def row_sums(block, row, value):
        folded = value[:, 0:128]
        for i in range(1, n // 128):
            folded = folded + value[:, 128 * i : 128 * (i + 1)]
        sums = nt(jnp.ones((16, 128), BF16), folded.astype(BF16))
        blocks[block].bias[row : row + 1, 0 : value.shape[0]] = sums[0:1]

    def layer(block, depth):
        b, w = blocks[block], weights[block]
        h = b.h[depth - 1]
        zed = tn(w[(names.first, names.mid0, names.mid1, names.mid2)[depth - 1]][...], h[0 : h.shape[0] - 16, :])
        zed = zed + b.hid[:, depth - 1 : depth]
        sig = 0.5 * jnp.tanh(0.5 * zed) + 0.5
        out = zed * sig
        b.h[depth][0:512, :] = out.astype(BF16)
        b.d[depth - 1][...] = (sig + out * (1.0 - sig)).astype(BF16)

    def theta(block, k):
        return (tn(weights[block].theta[k], blocks[block].h[4][0:512, :]) + blocks[block].hid[:, 4 + k : 5 + k]).astype(BF16)

    def heads(block, theta_f):
        wide = tn(weights[block].fore[...], theta_f) + blocks[block].foreb[:, 0:1]
        row = label_row()
        chosen = jnp.zeros((64, n), F32)
        for g in range(4):
            chosen = chosen + jnp.where(row == g, wide[64 * g : 64 * (g + 1)], 0.0)
        return chosen * s.scored[...].astype(F32)

    def residual(block, theta_b):
        backcast = nn(weights[block].back[...], theta_b) + blocks[block].backb[:, 0:1]
        return (blocks[block].h[0][0:336, :].astype(F32) - backcast) * s.mask[...].astype(F32)

    def inward(block, depth, dh):
        d = blocks[block].d[depth - 1]
        d[...] = (dh * d[...].astype(F32)).astype(BF16)

    def layer_biases(block):
        b, w = blocks[block], weights[block]
        lines = [
            jnp.concatenate([w.hid[4 * k + i : 4 * k + i + 1, :] for i in range(4)], axis=1) for k in range(6)
        ]
        lines.append(jnp.zeros((2, 512), F32))
        b.hid[...] = jnp.concatenate(lines, axis=0).T

    def end_biases(block):
        b, w = blocks[block], weights[block]
        b.backb[...] = jnp.broadcast_to(w.backb[...], (8, 336)).T
        b.foreb[...] = jnp.broadcast_to(w.foreb[...], (8, 256)).T

    def label_row():
        return jnp.concatenate([s.label[i : i + 1, :] for i in range(label_rows)], axis=1)

    def run(task):
        one, two = blocks
        if task == LOAD:
            loads.look.wait()
            mask = s.observed[...].astype(F32).astype(BF16)
            s.mask[...] = mask
            loads.past.wait()
            one.h[0][0:336, :] = one.h[0][0:336, :] * mask
            wait_weights(0, names.hid)
            layer_biases(0)
        elif task in (Z1_0, Z2_0, Z3_0, Z4_0):
            depth = task - Z1_0 + 1
            if depth == 1:
                wait_weights(0, names.first, names.mid0)
            elif depth == 3:
                wait_weights(0, names.mid1, names.mid2)
            layer(0, depth)
        elif task in (Z1_1, Z2_1, Z3_1, Z4_1):
            depth = task - Z1_1 + 1
            if depth == 1:
                wait_weights(1, *range(10))
                layer_biases(1)
            layer(1, depth)
        elif task == GH_0:
            wait_weights(0, *late)
            for load in (loads.label, loads.scored, loads.adjp, loads.adjl):
                load.wait()
            for b in blocks:
                for h in b.h:
                    k = h.shape[0] - 16
                    h[k : k + 16, :] = jnp.ones((16, n), BF16)
                b.bias[...] = jnp.zeros((16, 512), F32)
            df = s.adjp[...].astype(F32) * s.scored[...].astype(F32)
            row = label_row()
            gh = jnp.concatenate([jnp.where(row == g, df, 0.0) for g in range(4)], axis=0)
            s.gh[...] = gh.astype(BF16)
            for block in range(2):
                row_sums(block, 7, gh)
            one.pp[512:1024, :] = nn(weights[0].fore[...], s.gh[...]).astype(BF16)
        elif task == GTF_0:
            store_with_bias(0, TF, nt(one.h[4][...], one.pp[512:1024, :]), 5)
        elif task == BACK_0:
            wait_weights(0, *late)
            end_biases(0)
            theta_b = theta(0, 0)
            one.pp[0:512, :] = theta_b
            two.h[0][0:336, :] = residual(0, theta_b).astype(BF16)
        elif task == PP_1:
            wait_weights(1, *range(10))
            gb = -(two.gb[...] * s.mask[...])
            two.gb[...] = gb
            row_sums(1, 6, gb.astype(F32))
            two.pp[0:512, :] = tn(weights[1].back[...], gb).astype(BF16)
            two.pp[512:1024, :] = nn(weights[1].fore[...], s.gh[...]).astype(BF16)
        elif task == GT_1:
            store_with_bias(1, TB, nt(two.h[4][...], two.pp[0:512, :]), 4)
        elif task == GTF_1:
            store_with_bias(1, TF, nt(two.h[4][...], two.pp[512:1024, :]), 5)
        elif task in (DH4_1, DH4_0):
            block = int(task == DH4_1)
            pp, w = blocks[block].pp, weights[block]
            inward(block, 4, nn(w.theta[0], pp[0:512, :]) + nn(w.theta[1], pp[512:1024, :]))
        elif task in (B3_1, B2_1, B1_1, B3_0, B2_0, B1_0):
            block = int(task < GB_0)
            depth = 4 - (task - (B3_1 if block else B3_0))
            b, w = blocks[block], weights[block]
            dz = b.d[depth - 1][...]
            store_with_bias(block, (M0, M1, M2)[depth - 2], nt(b.h[depth - 1][...], dz), depth - 1)
            inward(block, depth - 1, nn(w[names.mid0 + depth - 2][...], dz))
        elif task in (B0_1, B0_0):
            block = int(task == B0_1)
            b = blocks[block]
            dz = b.d[0][...]
            store_with_bias(block, FIRST, nt(b.h[0][...], dz), 0)
            number, first = place_of(block, FIRST)
            rounds[number].part[first + 336 : first + 352, :] = b.bias[...].astype(BF16)
            direct = b.gb[...].astype(F32)
            din = (nn(weights[block].first[...], dz) - direct) * s.mask[...].astype(F32)
            if block:
                one.gb[...] = -(din.astype(BF16))
            else:
                s.dinput[...] = din.astype(BF16)
                hand_over(2)
        elif task == GB_0:
            gb = one.gb[...]
            row_sums(0, 6, gb.astype(F32))
            store(0, BACK, nt(gb, one.pp[0:512, :]))
            one.pp[0:512, :] = tn(weights[0].back[...], gb).astype(BF16)
        elif task == GTB_0:
            store_with_bias(0, TB, nt(one.h[4][...], one.pp[0:512, :]), 4)
        elif task == HEADS_0:
            theta_f = theta(0, 1)
            store(0, FORE, nt(theta_f, s.gh[...]))
            s.sent[...] = heads(0, theta_f).astype(BF16)
            hand_over(0)
        elif task == THETA_1:
            end_biases(1)
            for k in range(2):
                s.tt[512 * k : 512 * (k + 1), :] = theta(1, k)
            store(1, BACK, nt(two.gb[...], s.tt[0:512, :]))
            store(1, FORE, nt(s.tt[512:1024, :], s.gh[...]))
        else:
            s.total[...] = (s.sent[...].astype(F32) + heads(1, s.tt[512:1024, :])).astype(BF16)
            hand_over(1)
            s.r2[...] = residual(1, s.tt[0:512, :]).astype(BF16)
            hand_over(3)

    def fetch(*keys):
        for block in range(2):

            @pl.when(c == block)
            def _(block=block):
                for key in keys:
                    weight_local(block, key).start()

    def send_weights(*keys):
        for block in range(2):

            @pl.when(c == block)
            def _(block=block):
                for key in keys:
                    weight_remote(block, key).start()

    loads.look.start()
    loads.past.start()
    barrier = pltpu.get_barrier_semaphore()
    greeted = [(other, dp, y)]
    if whole:
        greeted += [(c, *place) for place in chips] + [(other, *place) for place in chips[:FAR]]
    for device in greeted:
        pl.semaphore_signal(barrier, inc=1, device_id=device, device_id_type=MESH)
    fetch(names.first, names.hid, names.mid0)
    pl.semaphore_wait(barrier, len(greeted))
    send_weights(names.first, names.hid, names.mid0)
    late = (names.fore, names.theta, names.back, names.backb, names.foreb)
    after = {LOAD: ((names.mid1, names.mid2, *late), (names.mid1, names.mid2)), Z2_0: ((), late)}

    sent = set()
    for item in ORDER:
        if item < STEP:
            run(item)
            if item in after:
                fetch(*after[item][0])
                send_weights(*after[item][1])
            if item == LOAD:
                for load in (loads.label, loads.scored, loads.adjp, loads.adjl):
                    load.start()
            for number in range(len(ROUNDS)):
                if not missing[number] and number not in sent:
                    sent.add(number)
                    message(number, c, D2D).start()
        elif whole:
            number, kind = (item - STEP) // 10, (item - STEP) % 10
            on_each_core(lambda core: step(number, core, kind))
    if not whole:
        for number in range(len(ROUNDS)):
            on_each_core(lambda core: chip_step(number, core))

    on_each_core(gathered_all)
    on_each_core(wait_sends)
    for key in range(10):
        for block in range(2):
            pl.when(c == block)(lambda block=block, key=key: weight_remote(block, key).wait_send())
    handed_over()


class Final(NamedTuple):
    pair: Any
    outcome: Any
    first: Any
    mid: Any
    theta: Any
    back: Any
    fore: Any
    hid: Any
    backb: Any
    foreb: Any


def widen(treedef, *refs):
    held, outs, wide, sem = jax.tree.unflatten(treedef, refs)
    leaving = []

    def leave(ref, out):
        copy = pltpu.make_async_copy(ref, out, sem.at[len(leaving)])
        copy.start()
        leaving.append(copy)

    def take(block):
        parts = parts_of(block)
        for i, part in enumerate(parts):
            number, core, low, count, piece, first = part
            source = held.rounds[number].own if core == block else held.rounds[number].rest
            rows = source[low : low + count, :].astype(F32)
            ref, out = (
                (wide.back, outs.back),
                (wide.fore, outs.fore),
                *((wide.theta.at[k], outs.theta.at[k]) for k in range(2)),
                *((wide.mid.at[k], outs.mid.at[k]) for k in range(3)),
                (wide.first, outs.first),
            )[piece]
            if piece == FORE:
                k = int(parts[i - 1] == part)
                ref[256 * k + first : 256 * k + first + count, :] = rows[:, 256 * k : 256 * (k + 1)]
            elif piece == FIRST:
                used = min(count, 336 - first)
                ref[first : first + used, :] = rows[:used]
                if used < count:
                    lines = rows[used : used + 8]
                    for k in range(24):
                        at = k % 4 * 128
                        wide.hid[k : k + 1, :] = lines[k // 4 : k // 4 + 1, at : at + 128]
                    wide.backb[...] = lines[6:7, 0:336]
                    wide.foreb[...] = lines[7:8, 0:256]
                    for one, two in ((wide.hid, outs.hid), (wide.backb, outs.backb), (wide.foreb, outs.foreb)):
                        leave(one, two)
            else:
                ref[first : first + count, :] = rows
            if not any(later[4] == piece for later in parts[i + 1 :]):
                leave(ref, out)

    def all_of(block):
        leaving.clear()
        for k in range(3):
            some = pl.ds(112 * k, 112)
            wide.outcome[some, :] = held.outcome[some, :].astype(F32)
            leave(wide.outcome.at[some], outs.outcome.at[some])
        wide.pair[...] = held.pair[...].astype(F32)
        leave(wide.pair, outs.pair)
        take(block)
        for copy in leaving:
            copy.wait()

    c = lax.axis_index("section")
    for block in range(2):
        pl.when(c == block)(functools.partial(all_of, block))


def shards(whole, past, label, look, scored, adjp, adjl, first, mid, theta, back, fore, hid, backb, foreb):
    windows = past.shape[0]
    n = windows // 2
    hbm = pl.BlockSpec(memory_space=pl.ANY)
    shape = jax.ShapeDtypeStruct
    inputs = Inputs(past.T, look.T, label.reshape(windows // 128, 128), scored.T, adjp.T, adjl.T)
    given = Given(first, mid, theta, back[0].T, fore, hid.reshape(24, 128), backb, foreb)
    results = Results(
        pair=pltpu.VMEM((64, windows), BF16),
        outcome=pltpu.VMEM((336, windows), BF16),
        rounds=[
            Gathered(*[pltpu.VMEM((rows_of(number) // 2, 512), BF16)] * 2) for number in range(len(ROUNDS))
        ],
    )
    buffers = jax.tree.leaves(scratch(n))
    treedef = jax.tree.structure((inputs, given, results, scratch(n)))
    near = pl.BlockSpec(memory_space=pltpu.VMEM)
    places = jax.tree.leaves(results)
    held = pl.pallas_call(
        functools.partial(body, n, whole, treedef),
        out_shape=places,
        in_specs=[hbm] * 14,
        out_specs=[near] * len(places),
        scratch_shapes=buffers,
        compiler_params=pltpu.CompilerParams(
            collective_id=0, has_side_effects=True, vmem_limit_bytes=54 * 2**20
        ),
    )(*inputs, *given)

    shapes = Final(
        pair=(64, windows),
        outcome=(336, windows),
        first=(336, 512),
        mid=(3, 512, 512),
        theta=(2, 512, 512),
        back=(336, 512),
        fore=(512, 256),
        hid=(24, 128),
        backb=(1, 336),
        foreb=(1, 256),
    )
    final = Final(*(shape(dims, F32) for dims in shapes))
    wide = Final(*(pltpu.VMEM(dims, F32) for dims in shapes))
    sem = pltpu.SemaphoreType.DMA((15,))
    treedef = jax.tree.structure((results, final, wide, sem))
    final = pl.pallas_call(
        functools.partial(widen, treedef),
        out_shape=final,
        in_specs=[near] * len(places),
        out_specs=Final(*[hbm] * 10),
        scratch_shapes=[*wide, sem],
        compiler_params=pltpu.CompilerParams(vmem_limit_bytes=32 * 2**20),
    )(*held)
    if not whole:
        final = Final(*final[:2], *lax.psum(tuple(final[2:]), ("dp", "rep")))
    return (
        final.pair.T[None],
        final.outcome.T[None],
        final.first[None],
        final.mid[None],
        final.theta[None],
        final.back.T[None],
        final.fore[None],
        final.hid.reshape(1, 6, 512),
        final.backb,
        final.foreb,
    )


def solution(mesh):
    wide = P(("dp", "rep"), None)
    s2, s3, s4 = (P("section", *([None] * k)) for k in (1, 2, 3))
    in_specs = (wide, P(("dp", "rep")), wide, wide, wide, wide, s3, s4, s4, s3, s3, s3, s2, s2)
    rowwise = P("section", ("dp", "rep"), None)
    out_specs = (rowwise, rowwise, s3, s4, s4, s3, s3, s3, s2, s2)
    whole = (mesh.shape["dp"], mesh.shape["rep"]) == (8, 2)
    run = functools.partial(shards, whole)
    return jax.shard_map(run, mesh=mesh, in_specs=in_specs, out_specs=out_specs, check_vma=False)
```

```python
import functools
from typing import Any, NamedTuple

import jax
import jax.numpy as jnp
from jax import lax
from jax.experimental import pallas as pl
from jax.experimental.pallas import tpu as pltpu
from jax.sharding import PartitionSpec as P

BF16 = jnp.bfloat16
F32 = jnp.float32
MESH = pl.DeviceIdType.MESH

BACK, FORE, TB, TF, M0, M1, M2, FIRST = range(8)
PIECE_ROWS = (384, 256, 512, 512, 512, 512, 512, 384)
ROUNDS = (
    (0, (TF,)),
    (1, (TB, TF,)),
    (1, (M2,)),
    (1, (M1,)),
    (1, (M0, FIRST,)),
    (1, (BACK, FORE,)),
    (0, (BACK, FORE, TB,)),
    (0, (M2,)),
    (0, (M1,)),
    (0, (M0,)),
    (0, (FIRST,)),
)
D2D, S1, S2, S3, S4, G3, G2, G1, G1X, GD = range(10)
X, Y, Z, FAR = range(4)
ROUTES = (
    ((X, Z, Y), (Y, X, Z)),
    ((Y, Z, X), (X, Y, Z)),
    ((Y, X, Z), (Y, X, Z)),
    ((X, Z, Y), (Z, Y, X)),
    ((Z, X, Y), (X, Y, Z)),
    ((Z, Y, X), (X, Y, Z)),
    ((Y, X, Z), (Z, Y, X)),
    ((Y, X, Z), (X, Z, Y)),
    ((Z, Y, X), (X, Y, Z)),
    ((X, Y, Z), (Y, X, Z)),
    ((Y, X, Z), (X, Y, Z)),
)
(
    LOAD, Z1_0, Z2_0, Z3_0, Z4_0, GH_0, GTF_0, BACK_0, Z1_1, Z2_1, Z3_1, Z4_1, PP_1, GT_1, DH4_1,
    B3_1, B2_1, B1_1, B0_1, GB_0, GTB_0, DH4_0, B3_0, B2_0, B1_0, B0_0, HEADS_0, THETA_1, FINAL_1, GTF_1,
) = range(30)
STEP = 1000
ORDER = (
    LOAD, Z1_0, Z2_0, Z3_0, Z4_0, BACK_0, Z1_1, GH_0, Z2_1, PP_1, Z3_1, Z4_1, GT_1, GTF_1, DH4_1, B3_1, 1010,
    B2_1, B1_1, B0_1, 1020, 1030, GB_0, 1011, 1040, HEADS_0, GTF_0, GTB_0, 1031, DH4_0, 1000, 1021, 1060,
    1012, THETA_1, 1041, B3_0, 1001, 1050, 1032, 1022, B2_0, 1070, 1061, 1013, B1_0, 1080, 1002, 1042, 1033,
    1051, FINAL_1, 1071, 1023, 1090, B0_0, 1062, 1014, 1081, 1003, 1100, 1052, 1043, 1024, 1091, 1072, 1034,
    1015, 1063, 1082, 1053, 1101, 1004, 1092, 1025, 1073, 1035, 1044, 1016, 1102, 1083, 1005, 1026, 1064,
    1093, 1054, 1036, 1045, 1103, 1074, 1006, 1084, 1065, 1094, 1055, 1104, 1046, 1075, 1085, 1095, 1066,
    1105, 1056, 1086, 1076, 1096, 1106,
)


def rows_of(number):
    return sum(PIECE_ROWS[piece] for piece in ROUNDS[number][1])


def place_of(block, piece):
    for number, (at, pieces) in enumerate(ROUNDS):
        if at == block and piece in pieces:
            return number, sum(PIECE_ROWS[p] for p in pieces[: pieces.index(piece)])


def rounds_of(block):
    return [number for number, (at, _) in enumerate(ROUNDS) if at == block]


def in_line(number, core):
    return ROUTES[number][core][2] == Z


def parts_of(block):
    parts = []
    for number, (at, pieces) in enumerate(ROUNDS):
        first = 0
        half = rows_of(number) // 2
        for piece in pieces if at == block else ():
            count = (336, 256, 512, 512, 512, 512, 512, 352)[piece]
            for core in range(2):
                low, high = max(first, core * half), min(first + count, (core + 1) * half)
                if low < high:
                    parts += [(number, core, low - core * half, high - low, piece, low - first)] * (1 + (piece == FORE))
            first += PIECE_ROWS[piece]
    return parts


def nn(a, b):
    return jnp.dot(a, b, preferred_element_type=F32)


def nt(a, b):
    return lax.dot_general(a, b, (((1,), (1,)), ((), ())), preferred_element_type=F32)


def tn(a, b):
    return lax.dot_general(a, b, (((0,), (0,)), ((), ())), preferred_element_type=F32)


class Inputs(NamedTuple):
    past: Any
    look: Any
    label: Any
    scored: Any
    adjp: Any
    adjl: Any


class Given(NamedTuple):
    first: Any
    mid: Any
    theta: Any
    back: Any
    fore: Any
    hid: Any
    backb: Any
    foreb: Any


class Gathered(NamedTuple):
    own: Any
    rest: Any


class Results(NamedTuple):
    pair: Any
    outcome: Any
    rounds: Any


class Weights(NamedTuple):
    first: Any
    hid: Any
    mid0: Any
    mid1: Any
    mid2: Any
    theta_b: Any
    theta_f: Any
    back: Any
    backb: Any
    fore: Any
    foreb: Any


class Block(NamedTuple):
    h: Any
    d: Any
    gb: Any
    pp: Any
    bias: Any
    hid: Any
    backb: Any
    foreb: Any


class Round(NamedTuple):
    part: Any
    landing: Any


class Scratch(NamedTuple):
    weights: Any
    blocks: Any
    rounds: Any
    observed: Any
    mask: Any
    label: Any
    scored: Any
    adjp: Any
    gh: Any
    tt: Any
    sent: Any
    total: Any
    dinput: Any
    r2: Any
    load_sem: Any
    weight_sem: Any
    weight_send: Any
    send_sem: Any
    recv_sem: Any
    out_send: Any
    last_send: Any
    last_recv: Any
    give_send: Any
    give_recv: Any


def scratch(n):
    def weights():
        square = pltpu.VMEM((512, 512), BF16)
        return Weights(
            first=pltpu.VMEM((336, 512), BF16),
            hid=pltpu.VMEM((24, 128), F32),
            mid0=square,
            mid1=square,
            mid2=square,
            theta_b=square,
            theta_f=square,
            back=pltpu.VMEM((336, 512), BF16),
            backb=pltpu.VMEM((1, 336), F32),
            fore=pltpu.VMEM((512, 256), BF16),
            foreb=pltpu.VMEM((1, 256), F32),
        )

    def block():
        return Block(
            h=[pltpu.VMEM(((336 if k == 0 else 512) + 16, n), BF16) for k in range(5)],
            d=[pltpu.VMEM((512, n), BF16) for _ in range(4)],
            gb=pltpu.VMEM((336, n), BF16),
            pp=pltpu.VMEM((1024, n), BF16),
            bias=pltpu.VMEM((16, 512), F32),
            hid=pltpu.VMEM((512, 8), F32),
            backb=pltpu.VMEM((336, 8), F32),
            foreb=pltpu.VMEM((256, 8), F32),
        )

    def a_round(number):
        rows = rows_of(number)
        half = rows // 2

        shapes = [(half, 512)]
        for _ in range(3):
            tall, wide = shapes[-1]
            shapes.append((tall // 2, wide) if tall // 2 % 16 == 0 else (tall, wide // 2))
        largest = shapes[2 if in_line(number, 0) or in_line(number, 1) else 3]
        shapes = [*shapes[:3], largest, largest]
        return Round(
            part=pltpu.VMEM((rows, 512), BF16),
            landing=[pltpu.VMEM(shape, BF16) for shape in shapes[1:]],
        )

    dma = pltpu.SemaphoreType.DMA
    count = len(ROUNDS)
    most = max(len(rounds_of(0)), len(rounds_of(1)))
    return Scratch(
        weights=[weights(), weights()],
        blocks=[block(), block()],
        rounds=[a_round(number) for number in range(count)],
        observed=pltpu.VMEM((336, n), jnp.int32),
        mask=pltpu.VMEM((336, n), BF16),
        label=pltpu.VMEM((n // 128, 128), jnp.int32),
        scored=pltpu.VMEM((64, n), jnp.int32),
        adjp=pltpu.VMEM((64, n), BF16),
        gh=pltpu.VMEM((256, n), BF16),
        tt=pltpu.VMEM((1024, n), BF16),
        sent=pltpu.VMEM((64, n), BF16),
        total=pltpu.VMEM((64, n), BF16),
        dinput=pltpu.VMEM((336, n), BF16),
        r2=pltpu.VMEM((336, n), BF16),
        load_sem=dma((6,)),
        weight_sem=dma((2, 11)),
        weight_send=dma((11,)),
        send_sem=dma((count,)),
        recv_sem=dma((count, 5)),
        out_send=dma((count,)),
        last_send=dma((most,)),
        last_recv=dma((most, 2)),
        give_send=dma((4,)),
        give_recv=dma((4,)),
    )


def body(n, whole, treedef, *refs):
    inputs, given, outs, s = jax.tree.unflatten(treedef, refs)
    weights, blocks = s.weights, s.blocks
    rounds = [Round(r.part, [place.own, *r.landing]) for r, place in zip(s.rounds, outs.rounds)]

    c = lax.axis_index("section")
    dp = lax.axis_index("dp")
    y = lax.axis_index("rep")
    z = lax.div(dp, 2)
    x = lax.rem(dp, 2)
    other = 1 - c
    dpx = dp + 1 - 2 * x
    dpz = dp + 2 - 4 * lax.rem(z, 2)
    dpm = 2 * (3 - z) + x
    ry = 1 - y
    chips = ((dpx, y), (dp, ry), (dpz, y), (dpm, y))
    sides = (x, y, lax.rem(lax.div(z + 1, 2), 2))

    between = (z == 1) | (z == 2)
    ends = (z == 0) | (z == 3)

    mine = pl.ds(pl.multiple_of(c * n, 128), n)
    label_rows = n // 128
    loads = Inputs(
        past=(inputs.past.at[:, mine], blocks[0].h[0].at[pl.ds(0, 336)]),
        look=(inputs.look.at[:, mine], s.observed),
        label=(inputs.label.at[pl.ds(pl.multiple_of(c * label_rows, 8), label_rows)], s.label),
        scored=(inputs.scored.at[:, mine], s.scored),
        adjp=(inputs.adjp.at[:, mine], s.adjp),
        adjl=(inputs.adjl.at[:, mine], blocks[1].gb),
    )
    loads = Inputs(*(pltpu.make_async_copy(*pair, s.load_sem.at[i]) for i, pair in enumerate(loads)))
    sources = Weights(
        first=given.first.at[0],
        hid=given.hid,
        mid0=given.mid.at[0, 0],
        mid1=given.mid.at[0, 1],
        mid2=given.mid.at[0, 2],
        theta_b=given.theta.at[0, 0],
        theta_f=given.theta.at[0, 1],
        back=given.back,
        backb=given.backb,
        fore=given.fore.at[0],
        foreb=given.foreb,
    )

    def weight_local(block, i):
        return pltpu.make_async_copy(sources[i], weights[block][i], s.weight_sem.at[block, i])

    def weight_remote(block, i):
        return pltpu.make_async_remote_copy(
            sources[i],
            weights[block][i],
            s.weight_send.at[i],
            s.weight_sem.at[block, i],
            device_id=(other, dp, y),
            device_id_type=MESH,
        )

    names = Weights(*range(11))

    waited = set()

    def wait_weights(block, *keys):
        for key in keys:
            if (block, key) not in waited:
                waited.add((block, key))
                weight_local(block, key).wait()

    def regions(number, core, base):
        keep, give = [(base, rows_of(number) // 2, 0, 512)], [None]
        for axis in ROUTES[number][core]:
            row, rows, col, cols = keep[-1]
            bit = sides[axis]
            if rows // 2 % 16 == 0:
                rows = rows // 2
                keep.append((row + bit * rows, rows, col, cols))
                give.append((row + (1 - bit) * rows, rows, col, cols))
            else:
                cols = cols // 2
                keep.append((row, rows, col + bit * cols, cols))
                give.append((row, rows, col + (1 - bit) * cols, cols))

        def at(row, rows, col, cols):
            across = slice(None) if cols == 512 else pl.ds(pl.multiple_of(col, 128), cols)
            return (pl.ds(pl.multiple_of(row, 16), rows), across)

        return [at(*area) for area in keep], [area and at(*area) for area in give]

    def summed(number, core):
        return regions(number, core, core * (rows_of(number) // 2))

    def gathered(number, core):
        return regions(number, core, 0)[0]

    def landing(number, core, kind):
        ref = rounds[number].landing[kind]
        if kind < S3 or in_line(number, core):
            return ref
        rows, cols = rounds[number].landing[S2].shape
        rows, cols = (rows // 2, cols) if rows // 2 % 16 == 0 else (rows, cols // 2)
        return ref.at[pl.ds(0, rows), pl.ds(0, cols)]

    def message(number, core, kind):
        r = rounds[number]
        half = rows_of(number) // 2
        if kind == D2D:
            where = (pl.ds(pl.multiple_of((1 - core) * half, 16), half), slice(None))
            src, dst, device = r.part.at[where], r.landing[D2D], (1 - core, dp, y)
        elif kind == GD and not whole:
            src, dst, device = r.landing[D2D], outs.rounds[number].rest, (1 - core, dp, y)
        else:
            axes = (*ROUTES[number][core], FAR)
            stage = {G3: 2, G2: 1, G1: 0, G1X: 0, GD: 0}.get(kind, kind - S1)
            last = 2 if in_line(number, core) else 3
            if kind <= S4:
                keep, give = summed(number, core)
                src, dst = r.part.at[give[kind] if kind <= last else keep[last]], landing(number, core, kind)
            else:
                where = gathered(number, core)[min(stage + 1, last)]
                src = r.landing[D2D].at[where]
                dst = src if kind <= G1 else outs.rounds[number].rest.at[where]
            place = (dp, y) if kind == GD else chips[axes[stage]]
            device = (1 - core if kind >= G1X else core, *place)
        return pltpu.make_async_remote_copy(
            src, dst, *semaphores(number, core, kind), device_id=device, device_id_type=MESH
        )

    def semaphores(number, core, kind):
        place = rounds_of(ROUNDS[number][0]).index(number)
        send = s.send_sem.at[number]
        if kind == GD:
            send = s.last_send.at[place]
        elif kind == G3 and whole and in_line(number, core):
            send = s.out_send.at[number]
        if kind >= G1X:
            return send, s.last_recv.at[place, kind - G1X]
        return send, s.recv_sem.at[number, {G1: D2D, G2: S1, G3: S2}.get(kind, kind)]

    def begin(number, core, kind, before):
        message(number, core, before).wait_send()
        message(number, core, kind).start()

    def fold(number, core, kind, where, *buffer):
        part = rounds[number].part
        part[where] = part[where] + landing(number, core, kind)[buffer]

    def fold_and_send(number, core, kind):
        keep, give = summed(number, core)
        level = kind + 1
        bit = sides[ROUTES[number][core][kind]]
        rows, cols = rounds[number].landing[kind].shape

        def of_landing(bit):
            if rows // 2 % 16 == 0:
                return (pl.ds(pl.multiple_of(bit * (rows // 2), 16), rows // 2), slice(None))
            return (slice(None), pl.ds(pl.multiple_of(bit * (cols // 2), 128), cols // 2))

        fold(number, core, kind, give[level], *of_landing(1 - bit))
        begin(number, core, level, kind)
        fold(number, core, kind, keep[level], *of_landing(bit))

    def settle(number, core, level):
        r = rounds[number]
        here = gathered(number, core)[level]
        r.landing[D2D][here] = r.part[summed(number, core)[0][level]] + landing(number, core, S4)[...]

    def chip_step(number, core):
        block = ROUNDS[number][0]
        r = rounds[number]
        half = rows_of(number) // 2
        message(number, core, D2D).wait_recv()
        r.landing[D2D][...] = r.landing[D2D][...] + r.part[core * half : (core + 1) * half, :]
        message(number, core, D2D).wait_send()
        if core == block:
            message(number, 1 - core, GD).wait_recv()
        else:
            message(number, core, GD).start()

    def step(number, core, kind):
        block = ROUNDS[number][0]
        line = in_line(number, core)
        keep2 = summed(number, core)[0][2]
        if line and kind in (S3, S4):

            @pl.when(between)
            def _():
                message(number, core, kind).wait_recv()
                if kind == S3:
                    fold(number, core, S3, keep2, ...)
                    begin(number, core, S4, S2)
                else:
                    settle(number, core, 2)
                    message(number, core, G3).start()
                    begin(number, core, G2, S4)

        elif line and kind == G3:

            @pl.when(ends)
            def _():
                message(number, core, G3).wait_recv()
                begin(number, core, G2, S3)

        else:
            message(number, core, kind).wait_recv()
            if kind == S2 and line:
                fold(number, core, S2, keep2, ...)
                pl.when(ends)(lambda: begin(number, core, S3, S2))
            elif kind < S3:
                fold_and_send(number, core, kind)
            elif kind == S3:
                fold(number, core, kind, summed(number, core)[0][3], ...)
                begin(number, core, S4, S3)
            elif kind == S4:
                settle(number, core, 3)
                begin(number, core, G3, S4)
            elif kind == G3:
                begin(number, core, G2, G3)
            else:
                message(number, core, G2).wait_send()
                if core == block:
                    message(number, core, G1).start()
                else:
                    message(number, core, G1X).start()
                    message(number, core, GD).start()

    def gathered_all(core):
        for number in rounds_of(core) if whole else ():
            quarter = rows_of(number) // 4
            theirs = sides[ROUTES[number][1 - core][0]]
            for kind, ref, at in (
                (G1, rounds[number].landing[D2D], 1 - sides[ROUTES[number][core][0]]),
                (GD, outs.rounds[number].rest, theirs),
                (G1X, outs.rounds[number].rest, 1 - theirs),
            ):
                ref = ref.at[pl.ds(pl.multiple_of(at * quarter, 16), quarter)]
                pltpu.make_async_remote_copy(
                    ref, ref, *semaphores(number, core, kind), device_id=(other, dp, y), device_id_type=MESH
                ).wait_recv()

    def wait_sends(core):
        for number, (block, _) in enumerate(ROUNDS):
            if whole:
                message(number, core, G1 if core == block else G1X).wait_send()
                if in_line(number, core):
                    pl.when(between)(lambda number=number: message(number, core, G3).wait_send())
            if core != block:
                message(number, core, GD).wait_send()

    def on_each_core(do):
        for core in range(2):
            pl.when(c == core)(functools.partial(do, core))

    def result(i):
        src = (s.sent, s.total, s.dinput, s.r2)[i]
        dst = (outs.pair, outs.outcome)[i // 2].at[:, mine]
        local = pltpu.make_async_copy(src, dst, s.give_send.at[i])
        remote = pltpu.make_async_remote_copy(
            src, dst, s.give_send.at[i], s.give_recv.at[i], device_id=(other, dp, y), device_id_type=MESH
        )
        return i % 2, local, remote

    def hand_over(i):
        keeper, local, remote = result(i)
        pl.when(c == keeper)(lambda: local.start())
        pl.when(c != keeper)(lambda: remote.start())

    def handed_over():
        for i in range(4):
            keeper, local, remote = result(i)

            @pl.when(c == keeper)
            def _(local=local, remote=remote):
                local.wait()
                remote.wait_recv()

            pl.when(c != keeper)(lambda remote=remote: remote.wait_send())

    missing = [set(pieces) for _, pieces in ROUNDS]

    def store(block, piece, value):
        number, first = place_of(block, piece)
        missing[number].discard(piece)
        value = value.astype(BF16)
        part = rounds[number].part
        if piece == FORE:
            for k in range(2):
                part[first : first + 256, 256 * k : 256 * (k + 1)] = value[256 * k : 256 * (k + 1)]
        else:
            part[first : first + value.shape[0], :] = value

    def store_with_bias(block, piece, value, row):
        k = value.shape[0] - 16
        blocks[block].bias[row : row + 1, :] = value[k : k + 1]
        store(block, piece, value[:k])

    def row_sums(block, row, value):
        folded = value[:, 0:128]
        for i in range(1, n // 128):
            folded = folded + value[:, 128 * i : 128 * (i + 1)]
        sums = nt(jnp.ones((16, 128), BF16), folded.astype(BF16))
        blocks[block].bias[row : row + 1, 0 : value.shape[0]] = sums[0:1]

    def layer(block, depth):
        b, w = blocks[block], weights[block]
        h = b.h[depth - 1]
        zed = tn(w[(names.first, names.mid0, names.mid1, names.mid2)[depth - 1]][...], h[0 : h.shape[0] - 16, :])
        zed = zed + b.hid[:, depth - 1 : depth]
        sig = 0.5 * jnp.tanh(0.5 * zed) + 0.5
        out = zed * sig
        b.h[depth][0:512, :] = out.astype(BF16)
        b.d[depth - 1][...] = (sig + out * (1.0 - sig)).astype(BF16)

    def theta(block, k):
        return (tn(weights[block][names.theta_b + k][...], blocks[block].h[4][0:512, :]) + blocks[block].hid[:, 4 + k : 5 + k]).astype(BF16)

    def heads(block, theta_f):
        wide = tn(weights[block].fore[...], theta_f) + blocks[block].foreb[:, 0:1]
        row = label_row()
        chosen = jnp.zeros((64, n), F32)
        for g in range(4):
            chosen = chosen + jnp.where(row == g, wide[64 * g : 64 * (g + 1)], 0.0)
        return chosen * s.scored[...].astype(F32)

    def residual(block, theta_b):
        backcast = nn(weights[block].back[...], theta_b) + blocks[block].backb[:, 0:1]
        return (blocks[block].h[0][0:336, :].astype(F32) - backcast) * s.mask[...].astype(F32)

    def inward(block, depth, dh):
        d = blocks[block].d[depth - 1]
        d[...] = (dh * d[...].astype(F32)).astype(BF16)

    def layer_biases(block):
        b, w = blocks[block], weights[block]
        lines = [
            jnp.concatenate([w.hid[4 * k + i : 4 * k + i + 1, :] for i in range(4)], axis=1) for k in range(6)
        ]
        lines.append(jnp.zeros((2, 512), F32))
        b.hid[...] = jnp.concatenate(lines, axis=0).T

    def end_biases(block):
        b, w = blocks[block], weights[block]
        b.backb[...] = jnp.broadcast_to(w.backb[...], (8, 336)).T
        b.foreb[...] = jnp.broadcast_to(w.foreb[...], (8, 256)).T

    def label_row():
        return jnp.concatenate([s.label[i : i + 1, :] for i in range(label_rows)], axis=1)

    def run(task):
        one, two = blocks
        if task == LOAD:
            loads.look.wait()
            mask = s.observed[...].astype(F32).astype(BF16)
            s.mask[...] = mask
            loads.past.wait()
            one.h[0][0:336, :] = one.h[0][0:336, :] * mask
            wait_weights(0, names.hid)
            layer_biases(0)
        elif task in (Z1_0, Z2_0, Z3_0, Z4_0):
            depth = task - Z1_0 + 1
            wait_weights(0, (names.first, names.mid0, names.mid1, names.mid2)[depth - 1])
            layer(0, depth)
        elif task in (Z1_1, Z2_1, Z3_1, Z4_1):
            depth = task - Z1_1 + 1
            if depth == 1:
                wait_weights(1, *range(11))
                layer_biases(1)
            layer(1, depth)
        elif task == GH_0:
            wait_weights(0, names.fore)
            for load in (loads.label, loads.scored, loads.adjp, loads.adjl):
                load.wait()
            for b in blocks:
                for h in b.h:
                    k = h.shape[0] - 16
                    h[k : k + 16, :] = jnp.ones((16, n), BF16)
                b.bias[...] = jnp.zeros((16, 512), F32)
            df = s.adjp[...].astype(F32) * s.scored[...].astype(F32)
            row = label_row()
            gh = jnp.concatenate([jnp.where(row == g, df, 0.0) for g in range(4)], axis=0)
            s.gh[...] = gh.astype(BF16)
            for block in range(2):
                row_sums(block, 7, gh)
            one.pp[512:1024, :] = nn(weights[0].fore[...], s.gh[...]).astype(BF16)
        elif task == GTF_0:
            store_with_bias(0, TF, nt(one.h[4][...], one.pp[512:1024, :]), 5)
        elif task == BACK_0:
            wait_weights(0, *late[:-1])
            end_biases(0)
            theta_b = theta(0, 0)
            one.pp[0:512, :] = theta_b
            two.h[0][0:336, :] = residual(0, theta_b).astype(BF16)
        elif task == PP_1:
            wait_weights(1, *range(11))
            gb = -(two.gb[...] * s.mask[...])
            two.gb[...] = gb
            row_sums(1, 6, gb.astype(F32))
            two.pp[0:512, :] = tn(weights[1].back[...], gb).astype(BF16)
            two.pp[512:1024, :] = nn(weights[1].fore[...], s.gh[...]).astype(BF16)
        elif task == GT_1:
            store_with_bias(1, TB, nt(two.h[4][...], two.pp[0:512, :]), 4)
        elif task == GTF_1:
            store_with_bias(1, TF, nt(two.h[4][...], two.pp[512:1024, :]), 5)
        elif task in (DH4_1, DH4_0):
            block = int(task == DH4_1)
            wait_weights(block, names.theta_f)
            pp, w = blocks[block].pp, weights[block]
            inward(block, 4, nn(w.theta_b[...], pp[0:512, :]) + nn(w.theta_f[...], pp[512:1024, :]))
        elif task in (B3_1, B2_1, B1_1, B3_0, B2_0, B1_0):
            block = int(task < GB_0)
            depth = 4 - (task - (B3_1 if block else B3_0))
            b, w = blocks[block], weights[block]
            dz = b.d[depth - 1][...]
            store_with_bias(block, (M0, M1, M2)[depth - 2], nt(b.h[depth - 1][...], dz), depth - 1)
            inward(block, depth - 1, nn(w[names.mid0 + depth - 2][...], dz))
        elif task in (B0_1, B0_0):
            block = int(task == B0_1)
            b = blocks[block]
            dz = b.d[0][...]
            store_with_bias(block, FIRST, nt(b.h[0][...], dz), 0)
            number, first = place_of(block, FIRST)
            rounds[number].part[first + 336 : first + 352, :] = b.bias[...].astype(BF16)
            direct = b.gb[...].astype(F32)
            din = (nn(weights[block].first[...], dz) - direct) * s.mask[...].astype(F32)
            if block:
                one.gb[...] = -(din.astype(BF16))
            else:
                s.dinput[...] = din.astype(BF16)
                hand_over(2)
        elif task == GB_0:
            gb = one.gb[...]
            row_sums(0, 6, gb.astype(F32))
            store(0, BACK, nt(gb, one.pp[0:512, :]))
            one.pp[0:512, :] = tn(weights[0].back[...], gb).astype(BF16)
        elif task == GTB_0:
            store_with_bias(0, TB, nt(one.h[4][...], one.pp[0:512, :]), 4)
        elif task == HEADS_0:
            wait_weights(0, names.theta_f)
            theta_f = theta(0, 1)
            store(0, FORE, nt(theta_f, s.gh[...]))
            s.sent[...] = heads(0, theta_f).astype(BF16)
            hand_over(0)
        elif task == THETA_1:
            end_biases(1)
            for k in range(2):
                s.tt[512 * k : 512 * (k + 1), :] = theta(1, k)
            store(1, BACK, nt(two.gb[...], s.tt[0:512, :]))
            store(1, FORE, nt(s.tt[512:1024, :], s.gh[...]))
        else:
            s.total[...] = (s.sent[...].astype(F32) + heads(1, s.tt[512:1024, :])).astype(BF16)
            hand_over(1)
            s.r2[...] = residual(1, s.tt[0:512, :]).astype(BF16)
            hand_over(3)

    def fetch(*keys):
        for block in range(2):

            @pl.when(c == block)
            def _(block=block):
                for key in keys:
                    weight_local(block, key).start()

    def send_weights(block, *keys):
        @pl.when(c == block)
        def _():
            for key in keys:
                weight_remote(block, key).start()

    loads.look.start()
    loads.past.start()
    barrier = pltpu.get_barrier_semaphore()
    greeted = [(other, dp, y)]
    if whole:
        greeted += [(c, *place) for place in chips] + [(other, *place) for place in chips[:FAR]]
    for device in greeted:
        pl.semaphore_signal(barrier, inc=1, device_id=device, device_id_type=MESH)
    fetch(names.first, names.hid, names.mid0)
    pl.semaphore_wait(barrier, len(greeted))
    late = (names.fore, names.theta_b, names.back, names.backb, names.foreb, names.theta_f)
    send_weights(0, names.first, names.hid, names.mid0)
    send_weights(1, names.first, names.hid, names.mid0, names.mid1, names.mid2, *late)
    after = {LOAD: (names.mid1, names.mid2), Z2_0: late[:2], Z3_0: late[2:]}

    sent = set()
    for item in ORDER:
        if item < STEP:
            run(item)
            if item in after:
                send_weights(0, *after[item])
            if item == LOAD:
                fetch(names.mid1, names.mid2, *late)
                for load in (loads.label, loads.scored, loads.adjp, loads.adjl):
                    load.start()
            for number in range(len(ROUNDS)):
                if not missing[number] and number not in sent:
                    sent.add(number)
                    message(number, c, D2D).start()
        elif whole:
            number, kind = (item - STEP) // 10, (item - STEP) % 10
            on_each_core(lambda core: step(number, core, kind))
    if not whole:
        for number in range(len(ROUNDS)):
            on_each_core(lambda core: chip_step(number, core))

    on_each_core(gathered_all)
    on_each_core(wait_sends)
    for key in range(11):
        for block in range(2):
            pl.when(c == block)(lambda block=block, key=key: weight_remote(block, key).wait_send())
    handed_over()


class Final(NamedTuple):
    pair: Any
    outcome: Any
    first: Any
    mid: Any
    theta: Any
    back: Any
    fore: Any
    hid: Any
    backb: Any
    foreb: Any


def widen(treedef, *refs):
    held, outs, wide, sem = jax.tree.unflatten(treedef, refs)
    leaving = []

    def leave(ref, out):
        copy = pltpu.make_async_copy(ref, out, sem.at[len(leaving)])
        copy.start()
        leaving.append(copy)

    def take(block):
        parts = parts_of(block)
        for i, part in enumerate(parts):
            number, core, low, count, piece, first = part
            source = held.rounds[number].own if core == block else held.rounds[number].rest
            rows = source[low : low + count, :].astype(F32)
            ref, out = (
                (wide.back, outs.back),
                (wide.fore, outs.fore),
                *((wide.theta.at[k], outs.theta.at[k]) for k in range(2)),
                *((wide.mid.at[k], outs.mid.at[k]) for k in range(3)),
                (wide.first, outs.first),
            )[piece]
            if piece == FORE:
                k = int(parts[i - 1] == part)
                ref[256 * k + first : 256 * k + first + count, :] = rows[:, 256 * k : 256 * (k + 1)]
            elif piece == FIRST:
                used = min(count, 336 - first)
                ref[first : first + used, :] = rows[:used]
                if used < count:
                    lines = rows[used : used + 8]
                    for k in range(24):
                        at = k % 4 * 128
                        wide.hid[k : k + 1, :] = lines[k // 4 : k // 4 + 1, at : at + 128]
                    wide.backb[...] = lines[6:7, 0:336]
                    wide.foreb[...] = lines[7:8, 0:256]
                    for one, two in ((wide.hid, outs.hid), (wide.backb, outs.backb), (wide.foreb, outs.foreb)):
                        leave(one, two)
            else:
                ref[first : first + count, :] = rows
            if not any(later[4] == piece for later in parts[i + 1 :]):
                leave(ref, out)

    def all_of(block):
        leaving.clear()
        for k in range(3):
            some = pl.ds(112 * k, 112)
            wide.outcome[some, :] = held.outcome[some, :].astype(F32)
            leave(wide.outcome.at[some], outs.outcome.at[some])
        wide.pair[...] = held.pair[...].astype(F32)
        leave(wide.pair, outs.pair)
        take(block)
        for copy in leaving:
            copy.wait()

    c = lax.axis_index("section")
    for block in range(2):
        pl.when(c == block)(functools.partial(all_of, block))


def shards(whole, past, label, look, scored, adjp, adjl, first, mid, theta, back, fore, hid, backb, foreb):
    windows = past.shape[0]
    n = windows // 2
    hbm = pl.BlockSpec(memory_space=pl.ANY)
    shape = jax.ShapeDtypeStruct
    inputs = Inputs(past.T, look.T, label.reshape(windows // 128, 128), scored.T, adjp.T, adjl.T)
    given = Given(first, mid, theta, back[0].T, fore, hid.reshape(24, 128), backb, foreb)
    results = Results(
        pair=pltpu.VMEM((64, windows), BF16),
        outcome=pltpu.VMEM((336, windows), BF16),
        rounds=[
            Gathered(*[pltpu.VMEM((rows_of(number) // 2, 512), BF16)] * 2) for number in range(len(ROUNDS))
        ],
    )
    buffers = jax.tree.leaves(scratch(n))
    treedef = jax.tree.structure((inputs, given, results, scratch(n)))
    near = pl.BlockSpec(memory_space=pltpu.VMEM)
    places = jax.tree.leaves(results)
    held = pl.pallas_call(
        functools.partial(body, n, whole, treedef),
        out_shape=places,
        in_specs=[hbm] * 14,
        out_specs=[near] * len(places),
        scratch_shapes=buffers,
        compiler_params=pltpu.CompilerParams(
            collective_id=0, has_side_effects=True, vmem_limit_bytes=54 * 2**20
        ),
    )(*inputs, *given)

    shapes = Final(
        pair=(64, windows),
        outcome=(336, windows),
        first=(336, 512),
        mid=(3, 512, 512),
        theta=(2, 512, 512),
        back=(336, 512),
        fore=(512, 256),
        hid=(24, 128),
        backb=(1, 336),
        foreb=(1, 256),
    )
    final = Final(*(shape(dims, F32) for dims in shapes))
    wide = Final(*(pltpu.VMEM(dims, F32) for dims in shapes))
    sem = pltpu.SemaphoreType.DMA((15,))
    treedef = jax.tree.structure((results, final, wide, sem))
    final = pl.pallas_call(
        functools.partial(widen, treedef),
        out_shape=final,
        in_specs=[near] * len(places),
        out_specs=Final(*[hbm] * 10),
        scratch_shapes=[*wide, sem],
        compiler_params=pltpu.CompilerParams(vmem_limit_bytes=32 * 2**20),
    )(*held)
    if not whole:
        final = Final(*final[:2], *lax.psum(tuple(final[2:]), ("dp", "rep")))
    return (
        final.pair.T[None],
        final.outcome.T[None],
        final.first[None],
        final.mid[None],
        final.theta[None],
        final.back.T[None],
        final.fore[None],
        final.hid.reshape(1, 6, 512),
        final.backb,
        final.foreb,
    )


def solution(mesh):
    wide = P(("dp", "rep"), None)
    s2, s3, s4 = (P("section", *([None] * k)) for k in (1, 2, 3))
    in_specs = (wide, P(("dp", "rep")), wide, wide, wide, wide, s3, s4, s4, s3, s3, s3, s2, s2)
    rowwise = P("section", ("dp", "rep"), None)
    out_specs = (rowwise, rowwise, s3, s4, s4, s3, s3, s3, s2, s2)
    whole = (mesh.shape["dp"], mesh.shape["rep"]) == (8, 2)
    run = functools.partial(shards, whole)
    return jax.shard_map(run, mesh=mesh, in_specs=in_specs, out_specs=out_specs, check_vma=False)
```

```python
import functools
from typing import Any, NamedTuple

import jax
import jax.numpy as jnp
from jax import lax
from jax.experimental import pallas as pl
from jax.experimental.pallas import tpu as pltpu
from jax.sharding import PartitionSpec as P

BF16 = jnp.bfloat16
F32 = jnp.float32
MESH = pl.DeviceIdType.MESH

BACK, FORE, TB, TF, M0, M1, M2, FIRST = range(8)
PIECE_ROWS = (384, 256, 512, 512, 512, 512, 512, 384)
ROUNDS = (
    (0, (TF,)),
    (1, (TB, TF,)),
    (1, (M2,)),
    (1, (M1,)),
    (1, (M0, FIRST,)),
    (1, (BACK, FORE,)),
    (0, (BACK, FORE, TB,)),
    (0, (M2,)),
    (0, (M1,)),
    (0, (M0,)),
    (0, (FIRST,)),
)
D2D, S1, S2, S3, S4, G3, G2, G1, G1X, GD = range(10)
X, Y, Z, FAR = range(4)
ROUTES = (
    ((X, Z, Y), (Y, X, Z)),
    ((Y, Z, X), (X, Y, Z)),
    ((Y, X, Z), (Y, X, Z)),
    ((X, Z, Y), (Z, Y, X)),
    ((Z, X, Y), (X, Y, Z)),
    ((Z, Y, X), (X, Y, Z)),
    ((Y, X, Z), (Z, Y, X)),
    ((Y, X, Z), (X, Z, Y)),
    ((Z, Y, X), (X, Y, Z)),
    ((X, Y, Z), (Y, X, Z)),
    ((Y, X, Z), (X, Y, Z)),
)
(
    LOAD, Z1_0, Z2_0, Z3_0, Z4_0, GH_0, GTF_0, BACK_0, Z1_1, Z2_1, Z3_1, Z4_1, PP_1, GT_1, DH4_1,
    B3_1, B2_1, B1_1, B0_1, GB_0, GTB_0, DH4_0, B3_0, B2_0, B1_0, B0_0, HEADS_0, THETA_1, FINAL_1, GTF_1,
) = range(30)
STEP = 1000
ORDER = (
    LOAD, Z1_0, Z2_0, Z3_0, Z4_0, BACK_0, Z1_1, GH_0, Z2_1, PP_1, Z3_1, Z4_1, GT_1, GTF_1, DH4_1, B3_1, 1010,
    B2_1, B1_1, B0_1, 1020, 1030, GB_0, 1011, 1040, HEADS_0, GTF_0, GTB_0, 1031, DH4_0, 1000, 1021, 1060,
    1012, THETA_1, 1041, B3_0, 1001, 1050, 1032, 1022, B2_0, 1070, 1061, 1013, B1_0, 1080, 1002, 1042, 1033,
    1051, FINAL_1, 1071, 1023, 1090, B0_0, 1062, 1014, 1081, 1003, 1100, 1052, 1043, 1024, 1091, 1072, 1034,
    1015, 1063, 1082, 1053, 1101, 1004, 1092, 1025, 1073, 1035, 1044, 1016, 1102, 1083, 1005, 1026, 1064,
    1093, 1054, 1036, 1045, 1103, 1074, 1006, 1084, 1065, 1094, 1055, 1104, 1046, 1075, 1085, 1095, 1066,
    1105, 1056, 1086, 1076, 1096, 1106,
)


def rows_of(number):
    return sum(PIECE_ROWS[piece] for piece in ROUNDS[number][1])


def place_of(block, piece):
    for number, (at, pieces) in enumerate(ROUNDS):
        if at == block and piece in pieces:
            return number, sum(PIECE_ROWS[p] for p in pieces[: pieces.index(piece)])


def rounds_of(block):
    return [number for number, (at, _) in enumerate(ROUNDS) if at == block]


def in_line(number, core):
    return ROUTES[number][core][2] == Z


def parts_of(block):
    parts = []
    for number, (at, pieces) in enumerate(ROUNDS):
        first = 0
        half = rows_of(number) // 2
        for piece in pieces if at == block else ():
            count = (336, 256, 512, 512, 512, 512, 512, 352)[piece]
            for core in range(2):
                low, high = max(first, core * half), min(first + count, (core + 1) * half)
                if low < high:
                    parts += [(number, core, low - core * half, high - low, piece, low - first)] * (1 + (piece == FORE))
            first += PIECE_ROWS[piece]
    return parts


def nn(a, b):
    return jnp.dot(a, b, preferred_element_type=F32)


def nt(a, b):
    return lax.dot_general(a, b, (((1,), (1,)), ((), ())), preferred_element_type=F32)


def tn(a, b):
    return lax.dot_general(a, b, (((0,), (0,)), ((), ())), preferred_element_type=F32)


class Inputs(NamedTuple):
    past: Any
    look: Any
    label: Any
    scored: Any
    adjp: Any
    adjl: Any


class Given(NamedTuple):
    first: Any
    mid: Any
    theta: Any
    back: Any
    fore: Any
    hid: Any
    backb: Any
    foreb: Any


class Gathered(NamedTuple):
    own: Any
    rest: Any


class Results(NamedTuple):
    pair: Any
    outcome: Any
    rounds: Any


class Weights(NamedTuple):
    first: Any
    hid: Any
    mid0: Any
    mid1: Any
    mid2: Any
    theta_b: Any
    theta_f: Any
    back: Any
    backb: Any
    fore: Any
    foreb: Any


class Block(NamedTuple):
    h: Any
    d: Any
    gb: Any
    pp: Any
    bias: Any
    hid: Any
    backb: Any
    foreb: Any


class Round(NamedTuple):
    part: Any
    landing: Any


class Scratch(NamedTuple):
    weights: Any
    blocks: Any
    rounds: Any
    observed: Any
    mask: Any
    label: Any
    scored: Any
    adjp: Any
    gh: Any
    tt: Any
    sent: Any
    total: Any
    dinput: Any
    r2: Any
    load_sem: Any
    weight_sem: Any
    weight_send: Any
    send_sem: Any
    recv_sem: Any
    out_send: Any
    last_send: Any
    last_recv: Any
    give_send: Any
    give_recv: Any


def scratch(n):
    def weights():
        square = pltpu.VMEM((512, 512), BF16)
        return Weights(
            first=pltpu.VMEM((336, 512), BF16),
            hid=pltpu.VMEM((24, 128), F32),
            mid0=square,
            mid1=square,
            mid2=square,
            theta_b=square,
            theta_f=square,
            back=pltpu.VMEM((336, 512), BF16),
            backb=pltpu.VMEM((1, 336), F32),
            fore=pltpu.VMEM((512, 256), BF16),
            foreb=pltpu.VMEM((1, 256), F32),
        )

    def block():
        return Block(
            h=[pltpu.VMEM(((336 if k == 0 else 512) + 16, n), BF16) for k in range(5)],
            d=[pltpu.VMEM((512, n), BF16) for _ in range(4)],
            gb=pltpu.VMEM((336, n), BF16),
            pp=pltpu.VMEM((1024, n), BF16),
            bias=pltpu.VMEM((16, 512), F32),
            hid=pltpu.VMEM((512, 8), F32),
            backb=pltpu.VMEM((336, 8), F32),
            foreb=pltpu.VMEM((256, 8), F32),
        )

    def a_round(number):
        rows = rows_of(number)
        half = rows // 2

        shapes = [(half, 512)]
        for _ in range(3):
            tall, wide = shapes[-1]
            shapes.append((tall // 2, wide) if tall // 2 % 16 == 0 else (tall, wide // 2))
        largest = shapes[2 if in_line(number, 0) or in_line(number, 1) else 3]
        shapes = [*shapes[:3], largest, largest]
        return Round(
            part=pltpu.VMEM((rows, 512), BF16),
            landing=[pltpu.VMEM(shape, BF16) for shape in shapes[1:]],
        )

    dma = pltpu.SemaphoreType.DMA
    count = len(ROUNDS)
    most = max(len(rounds_of(0)), len(rounds_of(1)))
    return Scratch(
        weights=[weights(), weights()],
        blocks=[block(), block()],
        rounds=[a_round(number) for number in range(count)],
        observed=pltpu.VMEM((336, n), jnp.int32),
        mask=pltpu.VMEM((336, n), BF16),
        label=pltpu.VMEM((n // 128, 128), jnp.int32),
        scored=pltpu.VMEM((64, n), jnp.int32),
        adjp=pltpu.VMEM((64, n), BF16),
        gh=pltpu.VMEM((256, n), BF16),
        tt=pltpu.VMEM((1024, n), BF16),
        sent=pltpu.VMEM((64, n), BF16),
        total=pltpu.VMEM((64, n), BF16),
        dinput=pltpu.VMEM((336, n), BF16),
        r2=pltpu.VMEM((336, n), BF16),
        load_sem=dma((6,)),
        weight_sem=dma((2, 11)),
        weight_send=dma((11,)),
        send_sem=dma((count,)),
        recv_sem=dma((count, 5)),
        out_send=dma((count,)),
        last_send=dma((most,)),
        last_recv=dma((most, 2)),
        give_send=dma((4,)),
        give_recv=dma((4,)),
    )


def body(n, whole, treedef, *refs):
    inputs, given, outs, s = jax.tree.unflatten(treedef, refs)
    weights, blocks = s.weights, s.blocks
    rounds = [Round(r.part, [place.own, *r.landing]) for r, place in zip(s.rounds, outs.rounds)]

    c = lax.axis_index("section")
    dp = lax.axis_index("dp")
    y = lax.axis_index("rep")
    z = lax.div(dp, 2)
    x = lax.rem(dp, 2)
    other = 1 - c
    dpx = dp + 1 - 2 * x
    dpz = dp + 2 - 4 * lax.rem(z, 2)
    dpm = 2 * (3 - z) + x
    ry = 1 - y
    chips = ((dpx, y), (dp, ry), (dpz, y), (dpm, y))
    sides = (x, y, lax.rem(lax.div(z + 1, 2), 2))

    between = (z == 1) | (z == 2)
    ends = (z == 0) | (z == 3)

    mine = pl.ds(pl.multiple_of(c * n, 128), n)
    label_rows = n // 128
    loads = Inputs(
        past=(inputs.past.at[:, mine], blocks[0].h[0].at[pl.ds(0, 336)]),
        look=(inputs.look.at[:, mine], s.observed),
        label=(inputs.label.at[pl.ds(pl.multiple_of(c * label_rows, 8), label_rows)], s.label),
        scored=(inputs.scored.at[:, mine], s.scored),
        adjp=(inputs.adjp.at[:, mine], s.adjp),
        adjl=(inputs.adjl.at[:, mine], blocks[1].gb),
    )
    loads = Inputs(*(pltpu.make_async_copy(*pair, s.load_sem.at[i]) for i, pair in enumerate(loads)))
    sources = Weights(
        first=given.first.at[0],
        hid=given.hid,
        mid0=given.mid.at[0, 0],
        mid1=given.mid.at[0, 1],
        mid2=given.mid.at[0, 2],
        theta_b=given.theta.at[0, 0],
        theta_f=given.theta.at[0, 1],
        back=given.back,
        backb=given.backb,
        fore=given.fore.at[0],
        foreb=given.foreb,
    )

    def weight_local(block, i):
        return pltpu.make_async_copy(sources[i], weights[block][i], s.weight_sem.at[block, i])

    def weight_remote(block, i):
        return pltpu.make_async_remote_copy(
            sources[i],
            weights[block][i],
            s.weight_send.at[i],
            s.weight_sem.at[block, i],
            device_id=(other, dp, y),
            device_id_type=MESH,
        )

    names = Weights(*range(11))

    waited = set()

    def wait_weights(block, *keys):
        for key in keys:
            if (block, key) not in waited:
                waited.add((block, key))
                weight_local(block, key).wait()

    def regions(number, core, base):
        keep, give = [(base, rows_of(number) // 2, 0, 512)], [None]
        for axis in ROUTES[number][core]:
            row, rows, col, cols = keep[-1]
            bit = sides[axis]
            if rows // 2 % 16 == 0:
                rows = rows // 2
                keep.append((row + bit * rows, rows, col, cols))
                give.append((row + (1 - bit) * rows, rows, col, cols))
            else:
                cols = cols // 2
                keep.append((row, rows, col + bit * cols, cols))
                give.append((row, rows, col + (1 - bit) * cols, cols))

        def at(row, rows, col, cols):
            across = slice(None) if cols == 512 else pl.ds(pl.multiple_of(col, 128), cols)
            return (pl.ds(pl.multiple_of(row, 16), rows), across)

        return [at(*area) for area in keep], [area and at(*area) for area in give]

    def summed(number, core):
        return regions(number, core, core * (rows_of(number) // 2))

    def gathered(number, core):
        return regions(number, core, 0)[0]

    def landing(number, core, kind):
        ref = rounds[number].landing[kind]
        if kind < S3 or in_line(number, core):
            return ref
        rows, cols = rounds[number].landing[S2].shape
        rows, cols = (rows // 2, cols) if rows // 2 % 16 == 0 else (rows, cols // 2)
        return ref.at[pl.ds(0, rows), pl.ds(0, cols)]

    def message(number, core, kind):
        r = rounds[number]
        half = rows_of(number) // 2
        if kind == D2D:
            where = (pl.ds(pl.multiple_of((1 - core) * half, 16), half), slice(None))
            src, dst, device = r.part.at[where], r.landing[D2D], (1 - core, dp, y)
        elif kind == GD and not whole:
            src, dst, device = r.landing[D2D], outs.rounds[number].rest, (1 - core, dp, y)
        else:
            axes = (*ROUTES[number][core], FAR)
            stage = {G3: 2, G2: 1, G1: 0, G1X: 0, GD: 0}.get(kind, kind - S1)
            last = 2 if in_line(number, core) else 3
            if kind <= S4:
                keep, give = summed(number, core)
                src, dst = r.part.at[give[kind] if kind <= last else keep[last]], landing(number, core, kind)
            else:
                where = gathered(number, core)[min(stage + 1, last)]
                src = r.landing[D2D].at[where]
                dst = src if kind <= G1 else outs.rounds[number].rest.at[where]
            place = (dp, y) if kind == GD else chips[axes[stage]]
            device = (1 - core if kind >= G1X else core, *place)
        return pltpu.make_async_remote_copy(
            src, dst, *semaphores(number, core, kind), device_id=device, device_id_type=MESH
        )

    def semaphores(number, core, kind):
        place = rounds_of(ROUNDS[number][0]).index(number)
        send = s.send_sem.at[number]
        if kind == GD:
            send = s.last_send.at[place]
        elif kind == G3 and whole and in_line(number, core):
            send = s.out_send.at[number]
        if kind >= G1X:
            return send, s.last_recv.at[place, kind - G1X]
        return send, s.recv_sem.at[number, {G1: D2D, G2: S1, G3: S2}.get(kind, kind)]

    def begin(number, core, kind, before):
        message(number, core, before).wait_send()
        message(number, core, kind).start()

    def fold(number, core, kind, where, *buffer):
        part = rounds[number].part
        part[where] = part[where] + landing(number, core, kind)[buffer]

    def fold_and_send(number, core, kind):
        keep, give = summed(number, core)
        level = kind + 1
        bit = sides[ROUTES[number][core][kind]]
        rows, cols = rounds[number].landing[kind].shape

        def of_landing(bit):
            if rows // 2 % 16 == 0:
                return (pl.ds(pl.multiple_of(bit * (rows // 2), 16), rows // 2), slice(None))
            return (slice(None), pl.ds(pl.multiple_of(bit * (cols // 2), 128), cols // 2))

        fold(number, core, kind, give[level], *of_landing(1 - bit))
        begin(number, core, level, kind)
        fold(number, core, kind, keep[level], *of_landing(bit))

    def settle(number, core, level):
        r = rounds[number]
        here = gathered(number, core)[level]
        r.landing[D2D][here] = r.part[summed(number, core)[0][level]] + landing(number, core, S4)[...]

    def chip_step(number, core):
        block = ROUNDS[number][0]
        r = rounds[number]
        half = rows_of(number) // 2
        message(number, core, D2D).wait_recv()
        r.landing[D2D][...] = r.landing[D2D][...] + r.part[core * half : (core + 1) * half, :]
        message(number, core, D2D).wait_send()
        if core == block:
            message(number, 1 - core, GD).wait_recv()
        else:
            message(number, core, GD).start()

    def step(number, core, kind):
        block = ROUNDS[number][0]
        line = in_line(number, core)
        keep2 = summed(number, core)[0][2]
        if line and kind in (S3, S4):

            @pl.when(between)
            def _():
                message(number, core, kind).wait_recv()
                if kind == S3:
                    fold(number, core, S3, keep2, ...)
                    begin(number, core, S4, S2)
                else:
                    settle(number, core, 2)
                    message(number, core, G3).start()
                    begin(number, core, G2, S4)

        elif line and kind == G3:

            @pl.when(ends)
            def _():
                message(number, core, G3).wait_recv()
                begin(number, core, G2, S3)

        else:
            message(number, core, kind).wait_recv()
            if kind == S2 and line:
                fold(number, core, S2, keep2, ...)
                pl.when(ends)(lambda: begin(number, core, S3, S2))
            elif kind < S3:
                fold_and_send(number, core, kind)
            elif kind == S3:
                fold(number, core, kind, summed(number, core)[0][3], ...)
                begin(number, core, S4, S3)
            elif kind == S4:
                settle(number, core, 3)
                begin(number, core, G3, S4)
            elif kind == G3:
                begin(number, core, G2, G3)
            else:
                message(number, core, G2).wait_send()
                if core == block:
                    message(number, core, G1).start()
                else:
                    message(number, core, G1X).start()
                    message(number, core, GD).start()

    def gathered_all(core):
        for number in rounds_of(core) if whole else ():
            quarter = rows_of(number) // 4
            theirs = sides[ROUTES[number][1 - core][0]]
            for kind, ref, at in (
                (G1, rounds[number].landing[D2D], 1 - sides[ROUTES[number][core][0]]),
                (GD, outs.rounds[number].rest, theirs),
                (G1X, outs.rounds[number].rest, 1 - theirs),
            ):
                ref = ref.at[pl.ds(pl.multiple_of(at * quarter, 16), quarter)]
                pltpu.make_async_remote_copy(
                    ref, ref, *semaphores(number, core, kind), device_id=(other, dp, y), device_id_type=MESH
                ).wait_recv()

    def wait_sends(core):
        for number, (block, _) in enumerate(ROUNDS):
            if whole:
                message(number, core, G1 if core == block else G1X).wait_send()
                if in_line(number, core):
                    pl.when(between)(lambda number=number: message(number, core, G3).wait_send())
            if core != block:
                message(number, core, GD).wait_send()

    def on_each_core(do):
        for core in range(2):
            pl.when(c == core)(functools.partial(do, core))

    def result(i):
        src = (s.sent, s.total, s.dinput, s.r2)[i]
        dst = (outs.pair, outs.outcome)[i // 2].at[:, mine]
        local = pltpu.make_async_copy(src, dst, s.give_send.at[i])
        remote = pltpu.make_async_remote_copy(
            src, dst, s.give_send.at[i], s.give_recv.at[i], device_id=(other, dp, y), device_id_type=MESH
        )
        return i % 2, local, remote

    def hand_over(i):
        keeper, local, remote = result(i)
        pl.when(c == keeper)(lambda: local.start())
        pl.when(c != keeper)(lambda: remote.start())

    def handed_over():
        for i in range(4):
            keeper, local, remote = result(i)

            @pl.when(c == keeper)
            def _(local=local, remote=remote):
                local.wait()
                remote.wait_recv()

            pl.when(c != keeper)(lambda remote=remote: remote.wait_send())

    missing = [set(pieces) for _, pieces in ROUNDS]

    def store(block, piece, value):
        number, first = place_of(block, piece)
        missing[number].discard(piece)
        value = value.astype(BF16)
        part = rounds[number].part
        if piece == FORE:
            for k in range(2):
                part[first : first + 256, 256 * k : 256 * (k + 1)] = value[256 * k : 256 * (k + 1)]
        else:
            part[first : first + value.shape[0], :] = value

    def store_with_bias(block, piece, value, row):
        k = value.shape[0] - 16
        blocks[block].bias[row : row + 1, :] = value[k : k + 1]
        store(block, piece, value[:k])

    def row_sums(block, row, value):
        folded = value[:, 0:128]
        for i in range(1, n // 128):
            folded = folded + value[:, 128 * i : 128 * (i + 1)]
        sums = nt(jnp.ones((16, 128), BF16), folded.astype(BF16))
        blocks[block].bias[row : row + 1, 0 : value.shape[0]] = sums[0:1]

    def layer(block, depth):
        b, w = blocks[block], weights[block]
        h = b.h[depth - 1]
        zed = tn(w[(names.first, names.mid0, names.mid1, names.mid2)[depth - 1]][...], h[0 : h.shape[0] - 16, :])
        zed = zed + b.hid[:, depth - 1 : depth]
        sig = 0.5 * jnp.tanh(0.5 * zed) + 0.5
        out = zed * sig
        b.h[depth][0:512, :] = out.astype(BF16)
        b.d[depth - 1][...] = (sig + out * (1.0 - sig)).astype(BF16)

    def theta(block, k):
        return (tn(weights[block][names.theta_b + k][...], blocks[block].h[4][0:512, :]) + blocks[block].hid[:, 4 + k : 5 + k]).astype(BF16)

    def heads(block, theta_f):
        wide = tn(weights[block].fore[...], theta_f) + blocks[block].foreb[:, 0:1]
        row = label_row()
        chosen = jnp.zeros((64, n), F32)
        for g in range(4):
            chosen = chosen + jnp.where(row == g, wide[64 * g : 64 * (g + 1)], 0.0)
        return chosen * s.scored[...].astype(F32)

    def residual(block, theta_b):
        backcast = nn(weights[block].back[...], theta_b) + blocks[block].backb[:, 0:1]
        return (blocks[block].h[0][0:336, :].astype(F32) - backcast) * s.mask[...].astype(F32)

    def inward(block, depth, dh):
        d = blocks[block].d[depth - 1]
        d[...] = (dh * d[...].astype(F32)).astype(BF16)

    def layer_biases(block):
        b, w = blocks[block], weights[block]
        lines = [
            jnp.concatenate([w.hid[4 * k + i : 4 * k + i + 1, :] for i in range(4)], axis=1) for k in range(6)
        ]
        lines.append(jnp.zeros((2, 512), F32))
        b.hid[...] = jnp.concatenate(lines, axis=0).T

    def end_biases(block):
        b, w = blocks[block], weights[block]
        b.backb[...] = jnp.broadcast_to(w.backb[...], (8, 336)).T
        b.foreb[...] = jnp.broadcast_to(w.foreb[...], (8, 256)).T

    def label_row():
        return jnp.concatenate([s.label[i : i + 1, :] for i in range(label_rows)], axis=1)

    def run(task):
        one, two = blocks
        if task == LOAD:
            loads.look.wait()
            mask = s.observed[...].astype(F32).astype(BF16)
            s.mask[...] = mask
            loads.past.wait()
            one.h[0][0:336, :] = one.h[0][0:336, :] * mask
            wait_weights(0, names.hid)
            layer_biases(0)
        elif task in (Z1_0, Z2_0, Z3_0, Z4_0):
            depth = task - Z1_0 + 1
            wait_weights(0, (names.first, names.mid0, names.mid1, names.mid2)[depth - 1])
            layer(0, depth)
        elif task in (Z1_1, Z2_1, Z3_1, Z4_1):
            depth = task - Z1_1 + 1
            if depth == 1:
                wait_weights(1, *range(11))
                layer_biases(1)
            layer(1, depth)
        elif task == GH_0:
            wait_weights(0, names.fore)
            for load in (loads.label, loads.scored, loads.adjp, loads.adjl):
                load.wait()
            for b in blocks:
                for h in b.h:
                    k = h.shape[0] - 16
                    h[k : k + 16, :] = jnp.ones((16, n), BF16)
                b.bias[...] = jnp.zeros((16, 512), F32)
            df = s.adjp[...].astype(F32) * s.scored[...].astype(F32)
            row = label_row()
            gh = jnp.concatenate([jnp.where(row == g, df, 0.0) for g in range(4)], axis=0)
            s.gh[...] = gh.astype(BF16)
            for block in range(2):
                row_sums(block, 7, gh)
            one.pp[512:1024, :] = nn(weights[0].fore[...], s.gh[...]).astype(BF16)
        elif task == GTF_0:
            store_with_bias(0, TF, nt(one.h[4][...], one.pp[512:1024, :]), 5)
        elif task == BACK_0:
            wait_weights(0, *late[:-1])
            end_biases(0)
            theta_b = theta(0, 0)
            one.pp[0:512, :] = theta_b
            two.h[0][0:336, :] = residual(0, theta_b).astype(BF16)
        elif task == PP_1:
            wait_weights(1, *range(11))
            gb = -(two.gb[...] * s.mask[...])
            two.gb[...] = gb
            row_sums(1, 6, gb.astype(F32))
            two.pp[0:512, :] = tn(weights[1].back[...], gb).astype(BF16)
            two.pp[512:1024, :] = nn(weights[1].fore[...], s.gh[...]).astype(BF16)
        elif task == GT_1:
            store_with_bias(1, TB, nt(two.h[4][...], two.pp[0:512, :]), 4)
        elif task == GTF_1:
            store_with_bias(1, TF, nt(two.h[4][...], two.pp[512:1024, :]), 5)
        elif task in (DH4_1, DH4_0):
            block = int(task == DH4_1)
            wait_weights(block, names.theta_f)
            pp, w = blocks[block].pp, weights[block]
            inward(block, 4, nn(w.theta_b[...], pp[0:512, :]) + nn(w.theta_f[...], pp[512:1024, :]))
        elif task in (B3_1, B2_1, B1_1, B3_0, B2_0, B1_0):
            block = int(task < GB_0)
            depth = 4 - (task - (B3_1 if block else B3_0))
            b, w = blocks[block], weights[block]
            dz = b.d[depth - 1][...]
            store_with_bias(block, (M0, M1, M2)[depth - 2], nt(b.h[depth - 1][...], dz), depth - 1)
            inward(block, depth - 1, nn(w[names.mid0 + depth - 2][...], dz))
        elif task in (B0_1, B0_0):
            block = int(task == B0_1)
            b = blocks[block]
            dz = b.d[0][...]
            store_with_bias(block, FIRST, nt(b.h[0][...], dz), 0)
            number, first = place_of(block, FIRST)
            rounds[number].part[first + 336 : first + 352, :] = b.bias[...].astype(BF16)
            direct = b.gb[...].astype(F32)
            din = (nn(weights[block].first[...], dz) - direct) * s.mask[...].astype(F32)
            if block:
                one.gb[...] = -(din.astype(BF16))
            else:
                s.dinput[...] = din.astype(BF16)
                hand_over(2)
        elif task == GB_0:
            gb = one.gb[...]
            row_sums(0, 6, gb.astype(F32))
            store(0, BACK, nt(gb, one.pp[0:512, :]))
            one.pp[0:512, :] = tn(weights[0].back[...], gb).astype(BF16)
        elif task == GTB_0:
            store_with_bias(0, TB, nt(one.h[4][...], one.pp[0:512, :]), 4)
        elif task == HEADS_0:
            wait_weights(0, names.theta_f)
            theta_f = theta(0, 1)
            store(0, FORE, nt(theta_f, s.gh[...]))
            s.sent[...] = heads(0, theta_f).astype(BF16)
            hand_over(0)
        elif task == THETA_1:
            end_biases(1)
            for k in range(2):
                s.tt[512 * k : 512 * (k + 1), :] = theta(1, k)
            store(1, BACK, nt(two.gb[...], s.tt[0:512, :]))
            store(1, FORE, nt(s.tt[512:1024, :], s.gh[...]))
        else:
            s.total[...] = (s.sent[...].astype(F32) + heads(1, s.tt[512:1024, :])).astype(BF16)
            hand_over(1)
            s.r2[...] = residual(1, s.tt[0:512, :]).astype(BF16)
            hand_over(3)

    def fetch(*keys):
        for block in range(2):

            @pl.when(c == block)
            def _(block=block):
                for key in keys:
                    weight_local(block, key).start()

    def send_weights(block, *keys):
        @pl.when(c == block)
        def _():
            for key in keys:
                weight_remote(block, key).start()

    loads.look.start()
    loads.past.start()
    barrier = pltpu.get_barrier_semaphore()
    greeted = [(other, dp, y)]
    if whole:
        greeted += [(c, *place) for place in chips] + [(other, *place) for place in chips[:FAR]]
    for device in greeted:
        pl.semaphore_signal(barrier, inc=1, device_id=device, device_id_type=MESH)
    pl.semaphore_wait(barrier, len(greeted))
    late = (names.fore, names.theta_b, names.back, names.backb, names.foreb, names.theta_f)
    send_weights(0, names.first, names.hid, names.mid0)
    fetch(names.first, names.hid, names.mid0)
    send_weights(1, names.first, names.hid, names.mid0, names.mid1, names.mid2)
    after = {LOAD: (names.mid1, names.mid2), Z2_0: late[:2], Z3_0: late[2:]}

    sent = set()
    for item in ORDER:
        if item < STEP:
            run(item)
            if item in after:
                send_weights(0, *after[item])
            if item == LOAD:
                fetch(names.mid1, names.mid2, *late)
                send_weights(1, *late)
                for load in (loads.label, loads.scored, loads.adjp, loads.adjl):
                    load.start()
            for number in range(len(ROUNDS)):
                if not missing[number] and number not in sent:
                    sent.add(number)
                    message(number, c, D2D).start()
        elif whole:
            number, kind = (item - STEP) // 10, (item - STEP) % 10
            on_each_core(lambda core: step(number, core, kind))
    if not whole:
        for number in range(len(ROUNDS)):
            on_each_core(lambda core: chip_step(number, core))

    on_each_core(gathered_all)
    on_each_core(wait_sends)
    for key in range(11):
        for block in range(2):
            pl.when(c == block)(lambda block=block, key=key: weight_remote(block, key).wait_send())
    handed_over()


class Final(NamedTuple):
    pair: Any
    outcome: Any
    first: Any
    mid: Any
    theta: Any
    back: Any
    fore: Any
    hid: Any
    backb: Any
    foreb: Any


def widen(treedef, *refs):
    held, outs, wide, sem = jax.tree.unflatten(treedef, refs)
    leaving = []

    def leave(ref, out):
        copy = pltpu.make_async_copy(ref, out, sem.at[len(leaving)])
        copy.start()
        leaving.append(copy)

    def take(block):
        parts = parts_of(block)
        for i, part in enumerate(parts):
            number, core, low, count, piece, first = part
            source = held.rounds[number].own if core == block else held.rounds[number].rest
            rows = source[low : low + count, :].astype(F32)
            ref, out = (
                (wide.back, outs.back),
                (wide.fore, outs.fore),
                *((wide.theta.at[k], outs.theta.at[k]) for k in range(2)),
                *((wide.mid.at[k], outs.mid.at[k]) for k in range(3)),
                (wide.first, outs.first),
            )[piece]
            if piece == FORE:
                k = int(parts[i - 1] == part)
                ref[256 * k + first : 256 * k + first + count, :] = rows[:, 256 * k : 256 * (k + 1)]
            elif piece == FIRST:
                used = min(count, 336 - first)
                ref[first : first + used, :] = rows[:used]
                if used < count:
                    lines = rows[used : used + 8]
                    for k in range(24):
                        at = k % 4 * 128
                        wide.hid[k : k + 1, :] = lines[k // 4 : k // 4 + 1, at : at + 128]
                    wide.backb[...] = lines[6:7, 0:336]
                    wide.foreb[...] = lines[7:8, 0:256]
                    for one, two in ((wide.hid, outs.hid), (wide.backb, outs.backb), (wide.foreb, outs.foreb)):
                        leave(one, two)
            else:
                ref[first : first + count, :] = rows
            if not any(later[4] == piece for later in parts[i + 1 :]):
                leave(ref, out)

    def all_of(block):
        leaving.clear()
        for k in range(3):
            some = pl.ds(112 * k, 112)
            wide.outcome[some, :] = held.outcome[some, :].astype(F32)
            leave(wide.outcome.at[some], outs.outcome.at[some])
        wide.pair[...] = held.pair[...].astype(F32)
        leave(wide.pair, outs.pair)
        take(block)
        for copy in leaving:
            copy.wait()

    c = lax.axis_index("section")
    for block in range(2):
        pl.when(c == block)(functools.partial(all_of, block))


def shards(whole, past, label, look, scored, adjp, adjl, first, mid, theta, back, fore, hid, backb, foreb):
    windows = past.shape[0]
    n = windows // 2
    hbm = pl.BlockSpec(memory_space=pl.ANY)
    shape = jax.ShapeDtypeStruct
    inputs = Inputs(past.T, look.T, label.reshape(windows // 128, 128), scored.T, adjp.T, adjl.T)
    given = Given(first, mid, theta, back[0].T, fore, hid.reshape(24, 128), backb, foreb)
    results = Results(
        pair=pltpu.VMEM((64, windows), BF16),
        outcome=pltpu.VMEM((336, windows), BF16),
        rounds=[
            Gathered(*[pltpu.VMEM((rows_of(number) // 2, 512), BF16)] * 2) for number in range(len(ROUNDS))
        ],
    )
    buffers = jax.tree.leaves(scratch(n))
    treedef = jax.tree.structure((inputs, given, results, scratch(n)))
    near = pl.BlockSpec(memory_space=pltpu.VMEM)
    places = jax.tree.leaves(results)
    held = pl.pallas_call(
        functools.partial(body, n, whole, treedef),
        out_shape=places,
        in_specs=[hbm] * 14,
        out_specs=[near] * len(places),
        scratch_shapes=buffers,
        compiler_params=pltpu.CompilerParams(
            collective_id=0, has_side_effects=True, vmem_limit_bytes=54 * 2**20
        ),
    )(*inputs, *given)

    shapes = Final(
        pair=(64, windows),
        outcome=(336, windows),
        first=(336, 512),
        mid=(3, 512, 512),
        theta=(2, 512, 512),
        back=(336, 512),
        fore=(512, 256),
        hid=(24, 128),
        backb=(1, 336),
        foreb=(1, 256),
    )
    final = Final(*(shape(dims, F32) for dims in shapes))
    wide = Final(*(pltpu.VMEM(dims, F32) for dims in shapes))
    sem = pltpu.SemaphoreType.DMA((15,))
    treedef = jax.tree.structure((results, final, wide, sem))
    final = pl.pallas_call(
        functools.partial(widen, treedef),
        out_shape=final,
        in_specs=[near] * len(places),
        out_specs=Final(*[hbm] * 10),
        scratch_shapes=[*wide, sem],
        compiler_params=pltpu.CompilerParams(vmem_limit_bytes=32 * 2**20),
    )(*held)
    if not whole:
        final = Final(*final[:2], *lax.psum(tuple(final[2:]), ("dp", "rep")))
    return (
        final.pair.T[None],
        final.outcome.T[None],
        final.first[None],
        final.mid[None],
        final.theta[None],
        final.back.T[None],
        final.fore[None],
        final.hid.reshape(1, 6, 512),
        final.backb,
        final.foreb,
    )


def solution(mesh):
    wide = P(("dp", "rep"), None)
    s2, s3, s4 = (P("section", *([None] * k)) for k in (1, 2, 3))
    in_specs = (wide, P(("dp", "rep")), wide, wide, wide, wide, s3, s4, s4, s3, s3, s3, s2, s2)
    rowwise = P("section", ("dp", "rep"), None)
    out_specs = (rowwise, rowwise, s3, s4, s4, s3, s3, s3, s2, s2)
    whole = (mesh.shape["dp"], mesh.shape["rep"]) == (8, 2)
    run = functools.partial(shards, whole)
    return jax.shard_map(run, mesh=mesh, in_specs=in_specs, out_specs=out_specs, check_vma=False)
```
